128 devices in a mesh: gx: 32 (over x, z, core), gz: 4 (over y).
Axes of the slice: x: 4, y: 4, z: 4, core: 2. Of those that a mesh axis runs over, the one named last changes fastest.
Arguments:
- density: bfloat16 [512, 128, 8192], P('gz', None, 'gx'), may hold values from 0 to 1
- tf_color: float32 [3, 8], replicated, may hold values from 0.2 to 1
- tf_extinction: float32 [8], replicated, may hold values from 0.8 to 6
Outputs:
- image: bfloat16 [4, 128, 8192], P(None, 'gz')
The draws below stay inside these ranges and needn't reach their ends.
All inputs are finite; a program needn't handle non-finite values.
Results may differ from the reference program's by a relative error of at most 0.0004.
Values may be sent and summed in bfloat16 or wider, within the bound.
A program may use at most 192 MiB of HBM per device.

```python
import math
import jax
import jax.numpy as jnp
from jax import lax

ZD = 128
ROWS = 128
XD = 256
KNOTS = 8
NZ = 512
NX = 8192


def draw_density(key, part):
    key = jax.random.fold_in(key, 11)
    cell_key, ray_key, plane_key = jax.random.split(key, 3)
    cellwise = jax.random.uniform(cell_key, (NZ, ROWS, NX), jnp.float32)
    planewise = jax.random.uniform(plane_key, (1, ROWS, NX), jnp.float32)
    raywise = jnp.exp(jax.random.uniform(ray_key, (1, ROWS, NX), jnp.float32, math.log(0.25), 0.0))
    return (raywise * (0.5 * cellwise + 0.5 * planewise)).astype(jnp.bfloat16)


def setup_inputs(seed: int = 0) -> dict:
    arg_keys = jax.random.split(jax.random.key(seed), 4)
    density = draw_density(jax.random.fold_in(arg_keys[3], 71), 0)
    tf_color = jnp.clip(jax.random.uniform(arg_keys[1], (3, KNOTS), jnp.float32, 0.2, 1.0), 0.2, 1.0)
    tf_extinction = jnp.clip(jnp.exp(jax.random.uniform(arg_keys[2], (KNOTS,), jnp.float32, math.log(0.8), math.log(6.0))), 0.8, 6.0)
    return {"density": density, "tf_color": tf_color, "tf_extinction": tf_extinction}


def shade_and_color(block, tf_color, tf_extinction):
    middle = block[:, :, 1:-1]
    slope_cols = 4.0 * (block[:, :, 2:] - block[:, :, :-2])
    padded_rows = jnp.pad(middle, ((0, 0), (1, 1), (0, 0)))
    slope_rows = 4.0 * (padded_rows[:, 2:, :] - padded_rows[:, :-2, :])
    shading = 0.5 + 0.5 * (0.6 * slope_cols + 0.8 * slope_rows) / jnp.sqrt(1.0 + slope_cols * slope_cols + slope_rows * slope_rows)
    levels = middle * (tf_extinction.shape[0] - 1)
    colors = [jnp.zeros_like(middle) for channel in range(3)]
    extinct = jnp.zeros_like(middle)
    for knot in range(tf_extinction.shape[0]):
        tent_weight = jnp.maximum(0.0, 1.0 - jnp.abs(levels - knot))
        colors = [colors[channel] + tent_weight * tf_color[channel, knot] for channel in range(3)]
        extinct = extinct + tent_weight * tf_extinction[knot]
    return (shading, colors, extinct)

def brick_strip(shading, colors, extinct, spacing):
    optical = extinct * spacing
    running = jnp.cumsum(optical, axis=0)
    emitted = jnp.exp(-(running - optical)) - jnp.exp(-running)
    lighted = emitted * shading
    planes = [lax.optimization_barrier(jnp.sum(lighted * colors[channel], axis=0)) for channel in range(3)]
    planes.append(1.0 - jnp.exp(-running[-1]))
    return jnp.stack(planes)

def reference(density, tf_color, tf_extinction):
    spacing = 1.0 / NZ
    bricks = NZ // ZD
    padded_full = jnp.pad(density.astype(jnp.float32), ((0, 0), (0, 0), (1, 1)))
    starts = jnp.arange(NX // XD, dtype=jnp.int32) * XD

    def one_block(start):
        block = lax.dynamic_slice_in_dim(padded_full, start.astype(jnp.int32), XD + 2, 2)
        shading, colors, extinct = shade_and_color(block, tf_color, tf_extinction)

        def split(field):
            return field.reshape(bricks, ZD, ROWS, XD)
        strips = jax.vmap(brick_strip, in_axes=(0, 0, 0, None))(split(shading), [split(c) for c in colors], split(extinct), spacing)
        clearance = 1.0 - strips[:, 3:4]
        ahead = jnp.concatenate([jnp.ones_like(clearance[:1]), jnp.cumprod(clearance, axis=0)[:-1]], axis=0)
        return lax.optimization_barrier(jnp.sum(ahead * strips, axis=0))
    blocks = lax.map(one_block, starts)
    whole = jnp.transpose(blocks, (1, 2, 0, 3)).reshape(4, ROWS, NX)
    return whole.astype(jnp.bfloat16)
```

```python
import functools
import math

import jax
import jax.numpy as jnp
from jax import lax
from jax.experimental import pallas as pl
from jax.experimental.pallas import tpu as pltpu
from jax.sharding import PartitionSpec as P

F32, BF16 = jnp.float32, jnp.bfloat16
MESH = pl.DeviceIdType.MESH
RU = 16
ZB = 8
ROUNDS = 2
GATHER = lax.GatherDimensionNumbers(
    offset_dims=(),
    collapsed_slice_dims=(0,),
    start_index_map=(0,),
    operand_batching_dims=(1,),
    start_indices_batching_dims=(1,),
)


def look(table, index):
    return lax.gather(
        table, index[..., None], GATHER, (1, 1), mode=lax.GatherScatterMode.PROMISE_IN_BOUNDS
    )


def dot(a, b):
    return jnp.dot(a, b, preferred_element_type=F32)


def iota(shape, dim):
    return lax.broadcasted_iota(jnp.int32, shape, dim)


def tables(tfc, tfe, total_depth):
    knots = tfe.shape[0]
    row = iota((8, 128), 0)
    found = []
    for fn in range(4):
        scale = 0.4 if fn < 3 else -math.log2(math.e) / total_depth
        value = [(tfc[fn, k] if fn < 3 else tfe[k]) * scale for k in range(knots)]
        a = jnp.zeros((8, 128), F32)
        b = jnp.zeros((8, 128), F32)
        for k in range(knots):
            if k + 1 < knots:
                rise = value[k + 1] - value[k]
                a = jnp.where(row == k, value[k] - rise * float(k), a)
                b = jnp.where(row == k, rise * float(knots - 1), b)
            else:
                a = jnp.where(row == k, value[k], a)
        found += [a, b]
    return found


def kernel(
    total_depth, den, tfc, tfe, out,
    D, onehot, edge, halo_in, halo, W, A, E, tab, pb0, rb0, pb1, rb1, strip, bricks, blk,
    load_sem, halo_ssem, halo_rsem, strip_ssem, strip_rsem, own_sem,
    a_ssem, a_rsem, b_ssem, b_rsem, c_ssem, c_rsem,
):
    gx, gz = lax.axis_index("gx"), lax.axis_index("gz")
    n_gx, n_gz = lax.axis_size("gx"), lax.axis_size("gz")
    depth, rows, cols = den.shape
    core, chip_z, chip_x = lax.rem(gx, 2), lax.rem(gx // 2, 4), gx // 8
    NZB, NLOAD = depth // ZB, depth // ZB
    HALF = depth // 2

    def gx_of(x, z, c):
        return x * 8 + z * 2 + c

    loads = [
        pltpu.make_async_copy(
            den.at[k * ZB : (k + 1) * ZB], D.at[k * ZB : (k + 1) * ZB, RU : RU + rows, :], load_sem.at[k]
        )
        for k in range(NLOAD)
    ]
    for copy in loads:
        copy.start()

    left, right = lax.rem(gx + n_gx - 1, n_gx), lax.rem(gx + 1, n_gx)
    sibling = (gx_of(chip_x, chip_z, 1 - core), gz)
    z_peers = [(gx_of(chip_x, lax.rem(chip_z + k, 4), core), gz) for k in (1, 2, 3)]
    x_peers = [(gx_of(lax.rem(chip_x + k, 4), chip_z, core), gz) for k in (1, 2, 3)]
    y_peers = [(gx, lax.rem(gz + k, n_gz)) for k in (1, 2, 3)]
    barrier = pltpu.get_barrier_semaphore()
    peers = [(left, gz), (right, gz), sibling] + z_peers + x_peers + y_peers
    for peer in peers:
        pl.semaphore_signal(barrier, inc=1, device_id=peer, device_id_type=MESH)

    D[:, 0:RU, :] = jnp.zeros((depth, RU, cols), BF16)
    D[:, RU + rows : 2 * RU + rows, :] = jnp.zeros((depth, RU, cols), BF16)
    lane = lax.rem(iota((RU, 128), 1), HALF)

    def mark(z, _):
        onehot[z] = jnp.where(lane == z, 1.0, 0.0).astype(BF16)
        return 0

    lax.fori_loop(0, HALF, mark, 0)
    k, x = iota((cols, cols), 0), iota((cols, cols), 1)
    W[0:cols, :] = (jnp.where(k == x + 1, 1.0, 0.0) - jnp.where(k == x - 1, 1.0, 0.0)).astype(BF16)
    k, x = iota((128, cols), 0), iota((128, cols), 1)
    W[cols : cols + 128, :] = (
        jnp.where((k < HALF) & (x == cols - 1), 1.0, 0.0) - jnp.where((k >= HALF) & (x == 0), 1.0, 0.0)
    ).astype(BF16)
    k, x = iota((cols, 128), 0), iota((cols, 128), 1)
    E[...] = jnp.where(((k == 0) & (x < HALF)) | ((k == cols - 1) & (x >= HALF)), 1.0, 0.0).astype(BF16)
    m, k = iota((4 * RU, 12 * RU), 0), iota((4 * RU, 12 * RU), 1)
    at = (m // RU) * (3 * RU) + RU + lax.rem(m, RU)
    A[...] = (jnp.where(k == at + 1, 1.0, 0.0) - jnp.where(k == at - 1, 1.0, 0.0)).astype(BF16)
    for n, t in enumerate(tables(tfc, tfe, total_depth)):
        tab[n] = t

    lane_all = lax.rem(iota((rows, 128), 1), HALF)
    for part in range(2):
        acc = jnp.zeros((rows, 128), F32)
        for k in range(NLOAD // 2 * part, NLOAD // 2 * (part + 1)):
            loads[k].wait()
            spread = dot(D[k * ZB : (k + 1) * ZB, RU : RU + rows, :].reshape(ZB * rows, cols), E[...])
            for j in range(ZB):
                acc = jnp.where(lane_all == k * ZB + j - part * HALF, spread[j * rows : (j + 1) * rows], acc)
        edge[part] = acc.astype(BF16)

    pl.semaphore_wait(barrier, len(peers))
    halo_copies = [
        pltpu.make_async_remote_copy(
            src_ref=edge, dst_ref=halo_in.at[side], send_sem=halo_ssem.at[side], recv_sem=halo_rsem.at[side],
            device_id=(target, gz), device_id_type=MESH,
        )
        for side, target in ((0, left), (1, right))
    ]
    for copy in halo_copies:
        copy.start()
    for copy in halo_copies:
        copy.wait()
    lane_halo = iota((rows, 128), 1)
    keep_right = jnp.where(gx == n_gx - 1, 0.0, 1.0)
    keep_left = jnp.where(gx == 0, 0.0, 1.0)
    for part in range(2):
        halo[part] = jnp.where(
            lane_halo < HALF,
            halo_in[0, part].astype(F32) * keep_right,
            halo_in[1, part].astype(F32) * keep_left,
        ).astype(BF16)

    def unit_rows(u):
        return pl.multiple_of(lax.rem(gz + 1 + lax.rem(u, 4), 4) * (2 * RU) + (u // 4) * RU, RU)

    def slopes(y0, zb, pb, rb):
        z0 = pl.multiple_of(zb * ZB, ZB)
        block = D[pl.ds(z0, ZB), pl.ds(RU + y0, RU), :].reshape(ZB * RU, cols)
        part = z0 // HALF
        edges = halo[part, pl.ds(y0, RU), :][None] * onehot[pl.ds(z0 - part * HALF, ZB)]
        pb[...] = dot(jnp.concatenate([block, edges.reshape(ZB * RU, 128)], 1), W[...])
        for i in range(ZB // 4):
            near = D[pl.ds(z0 + 4 * i, 4), pl.ds(y0, 3 * RU), :].reshape(12 * RU, cols)
            rb[4 * RU * i : 4 * RU * (i + 1), :] = dot(A[...], near)

    def march(y0, zb, pb, rb, carry):
        z0 = zb * ZB
        T = [tab[n] for n in range(8)]

        def step(z, carry):
            r0 = pl.multiple_of(z * RU, RU)
            dx, dy = pb[pl.ds(r0, RU)], rb[pl.ds(r0, RU)]
            dens = D[z0 + z, pl.ds(RU + y0, RU), :].astype(F32)
            new = []
            for k in range(4):
                i, j = k // 2, k % 2
                sl = (slice(8 * i, 8 * i + 8), slice(128 * j, 128 * j + 128))
                p, r, d = dx[sl], dy[sl], dens[sl]
                run, clear, red, green, blue = carry[5 * k : 5 * k + 5]
                q = (0.75 * p + r) * lax.rsqrt((p * p + 0.0625) + r * r)
                ix = (d * 7.0).astype(jnp.int32)
                run = (run + look(T[6], ix)) + look(T[7], ix) * d
                after = jnp.exp2(run)
                w = (clear - after) * (1.25 + q)
                red = red + w * (look(T[0], ix) + look(T[1], ix) * d)
                green = green + w * (look(T[2], ix) + look(T[3], ix) * d)
                blue = blue + w * (look(T[4], ix) + look(T[5], ix) * d)
                new += [run, after, red, green, blue]
            return tuple(new)

        return lax.fori_loop(0, ZB, step, carry, unroll=True)

    def strip_copy(u):
        slot = u // 4
        target = lax.rem(gz + 1 + lax.rem(u, 4), 4)
        return pltpu.make_async_remote_copy(
            src_ref=strip.at[u], dst_ref=bricks.at[slot, gz], send_sem=strip_ssem.at[u],
            recv_sem=strip_rsem.at[slot, gz], device_id=(gx, target), device_id_type=MESH,
        )

    def column(x, z):
        return pl.multiple_of(gx_of(x, z, core) * cols, cols)

    def place(h, p, x, z):
        return out.at[2 * p : 2 * p + 2, RU * h : RU * h + RU, pl.ds(column(x, z), cols)]

    def own_copy(h):
        return pltpu.make_async_copy(
            blk.at[h], out.at[:, RU * h : RU * h + RU, pl.ds(column(chip_x, chip_z), cols)], own_sem.at[h]
        )

    def a_copies(h):
        found = []
        for p, targets, me in ((0, z_peers, chip_z), (1, x_peers, chip_x)):
            for k, target in enumerate(targets):
                found.append(
                    pltpu.make_async_remote_copy(
                        src_ref=blk.at[h, 2 * p : 2 * p + 2], dst_ref=place(h, p, chip_x, chip_z),
                        send_sem=a_ssem.at[h, p, k], recv_sem=a_rsem.at[h, p, k],
                        device_id=target, device_id_type=MESH,
                    )
                )
        return found

    def b_copy(h, p, k, n, spot):
        return pltpu.make_async_remote_copy(
            src_ref=spot, dst_ref=spot, send_sem=b_ssem.at[h, p, k, n], recv_sem=b_rsem.at[h, p, k, n],
            device_id=(x_peers, z_peers)[p][k], device_id_type=MESH,
        )

    def b_copies(h):
        return [
            b_copy(h, p, k, n, place(h, p, n, chip_z) if p else place(h, p, chip_x, n))
            for p in range(2) for k in range(3) for n in range(4)
        ]

    def a_arrivals(h):
        found = []
        for p in range(2):
            for k in range(3):
                back = 3 - k
                x = lax.rem(chip_x + back, 4) if p else chip_x
                z = chip_z if p else lax.rem(chip_z + back, 4)
                spot = place(h, p, x, z)
                found.append(
                    pltpu.make_async_remote_copy(
                        src_ref=spot, dst_ref=spot, send_sem=a_ssem.at[h, p, k], recv_sem=a_rsem.at[h, p, k],
                        device_id=(z_peers, x_peers)[p][k], device_id_type=MESH,
                    )
                )
        return found

    def b_arrivals(h):
        found = []
        for k in range(3):
            x, z = lax.rem(chip_x + 3 - k, 4), lax.rem(chip_z + 3 - k, 4)
            for n in range(4):
                found += [b_copy(h, 0, k, n, place(h, 0, x, n)), b_copy(h, 1, k, n, place(h, 1, n, z))]
        return found

    def c_copies(h, c):
        found = []
        for chip in range(16):
            at = pl.multiple_of((2 * chip + c) * cols, cols)
            spot = out.at[:, RU * h : RU * h + RU, pl.ds(at, cols)]
            found.append(
                pltpu.make_async_remote_copy(
                    src_ref=spot, dst_ref=spot, send_sem=c_ssem.at[h, chip], recv_sem=c_rsem.at[h, chip],
                    device_id=sibling, device_id_type=MESH,
                )
            )
        return found

    def composite(h):
        for k in (1, 2, 3):
            brick = lax.rem(gz + k, 4)
            pltpu.make_async_remote_copy(
                src_ref=strip.at[0], dst_ref=bricks.at[h, brick], send_sem=strip_ssem.at[0],
                recv_sem=strip_rsem.at[h, brick], device_id=(gx, brick), device_id_type=MESH,
            ).wait_recv()
        ahead = bricks[h, 0, 3]
        total = [bricks[h, 0, c] for c in range(3)] + [1.0 - ahead]
        for b in range(1, 4):
            through = bricks[h, b, 3]
            total = [total[c] + ahead * bricks[h, b, c] for c in range(3)] + [total[3] + ahead * (1.0 - through)]
            ahead = ahead * through
        for c in range(4):
            blk[h, c] = total[c].astype(BF16)
        own_copy(h).start()
        for copy in a_copies(h):
            copy.start()

    def stage_b(h):
        own_copy(h).wait()
        for copy in a_arrivals(h):
            copy.wait_recv()
        for copy in b_copies(h):
            copy.start()

    def stage_c(h):
        for copy in b_arrivals(h):
            copy.wait_recv()
        for copy in c_copies(h, core):
            copy.start()

    def unit(u, _):
        y0 = unit_rows(u)
        zero, one = jnp.zeros((8, 128), F32), jnp.ones((8, 128), F32)
        slopes(y0, 0, pb0, rb0)

        def pair(i, carry):
            slopes(y0, 2 * i + 1, pb1, rb1)
            carry = march(y0, 2 * i, pb0, rb0, carry)
            slopes(y0, lax.rem(2 * i + 2, NZB), pb0, rb0)
            return march(y0, 2 * i + 1, pb1, rb1, carry)

        carry = lax.fori_loop(0, NZB // 2, pair, (zero, one, zero, zero, zero) * 4)

        def keep(ref):
            for k in range(4):
                i, j = k // 2, k % 2
                _, clear, red, green, blue = carry[5 * k : 5 * k + 5]
                for c, v in enumerate((red, green, blue, clear)):
                    ref[c, 8 * i : 8 * i + 8, 128 * j : 128 * j + 128] = v

        @pl.when(lax.rem(u, 4) < 3)
        def _():
            keep(strip.at[u])
            strip_copy(u).start()

        @pl.when(lax.rem(u, 4) == 3)
        def _():
            keep(bricks.at[u // 4, gz])

        @pl.when(u == 4)
        def _():
            composite(0)

        @pl.when(u == 5)
        def _():
            stage_b(0)

        @pl.when(u == 6)
        def _():
            stage_c(0)

        return 0

    lax.fori_loop(0, 4 * ROUNDS, unit, 0)
    composite(1)
    stage_b(1)
    stage_c(1)
    for h in range(ROUNDS):
        for copy in c_copies(h, 1 - core):
            copy.wait_recv()
        for copy in a_copies(h) + b_copies(h) + c_copies(h, core):
            copy.wait_send()
        for s in range(3):
            strip_copy(4 * h + s).wait_send()


def render(density, tf_color, tf_extinction):
    depth, rows, cols = density.shape
    n_gx, n_gz = lax.axis_size("gx"), lax.axis_size("gz")
    D = pltpu.SemaphoreType.DMA
    return pl.pallas_call(
        functools.partial(kernel, depth * n_gz),
        out_shape=jax.ShapeDtypeStruct((4, rows // n_gz, cols * n_gx), BF16),
        in_specs=[
            pl.BlockSpec(memory_space=pl.ANY),
            pl.BlockSpec(memory_space=pltpu.SMEM),
            pl.BlockSpec(memory_space=pltpu.SMEM),
        ],
        out_specs=pl.BlockSpec(memory_space=pl.ANY),
        scratch_shapes=[
            pltpu.VMEM((depth, rows + 2 * RU, cols), BF16),
            pltpu.VMEM((depth // 2, RU, 128), BF16),
            pltpu.VMEM((2, rows, 128), BF16),
            pltpu.VMEM((2, 2, rows, 128), BF16),
            pltpu.VMEM((2, rows, 128), BF16),
            pltpu.VMEM((cols + 128, cols), BF16),
            pltpu.VMEM((4 * RU, 12 * RU), BF16),
            pltpu.VMEM((cols, 128), BF16),
            pltpu.VMEM((8, 8, 128), F32),
            pltpu.VMEM((ZB * RU, cols), F32),
            pltpu.VMEM((ZB * RU, cols), F32),
            pltpu.VMEM((ZB * RU, cols), F32),
            pltpu.VMEM((ZB * RU, cols), F32),
            pltpu.VMEM((4 * ROUNDS, 4, RU, cols), F32),
            pltpu.VMEM((ROUNDS, 4, 4, RU, cols), F32),
            pltpu.VMEM((ROUNDS, 4, RU, cols), BF16),
            D((depth // ZB,)),
            D((2,)),
            D((2,)),
            D((4 * ROUNDS,)),
            D((ROUNDS, 4)),
            D((ROUNDS,)),
            D((ROUNDS, 2, 3)),
            D((ROUNDS, 2, 3)),
            D((ROUNDS, 2, 3, 4)),
            D((ROUNDS, 2, 3, 4)),
            D((ROUNDS, 16)),
            D((ROUNDS, 16)),
        ],
        compiler_params=pltpu.CompilerParams(
            collective_id=0, has_side_effects=True, vmem_limit_bytes=58 * 2**20
        ),
    )(density, tf_color, tf_extinction)


def solution(mesh):
    in_specs = (P("gz", None, "gx"), P(), P())
    return jax.shard_map(
        render, mesh=mesh, in_specs=in_specs, out_specs=P(None, "gz", None), check_vma=False
    )
```

```python
import functools
import math

import jax
import jax.numpy as jnp
from jax import lax
from jax.experimental import pallas as pl
from jax.experimental.pallas import tpu as pltpu
from jax.sharding import PartitionSpec as P

F32, BF16 = jnp.float32, jnp.bfloat16
MESH = pl.DeviceIdType.MESH
RU = 16
AHEAD = 4
ZB = 8
ROUNDS = 2
GATHER = lax.GatherDimensionNumbers(
    offset_dims=(),
    collapsed_slice_dims=(0,),
    start_index_map=(0,),
    operand_batching_dims=(1,),
    start_indices_batching_dims=(1,),
)


def look(table, index):
    return lax.gather(
        table, index[..., None], GATHER, (1, 1), mode=lax.GatherScatterMode.PROMISE_IN_BOUNDS
    )


def dot(a, b):
    return jnp.dot(a, b, preferred_element_type=F32)


def iota(shape, dim):
    return lax.broadcasted_iota(jnp.int32, shape, dim)


def tables(tfc, tfe, total_depth):
    knots = tfe.shape[0]
    row = iota((8, 128), 0)
    found = []
    for fn in range(4):
        scale = 0.4 if fn < 3 else -math.log2(math.e) / total_depth
        value = [(tfc[fn, k] if fn < 3 else tfe[k]) * scale for k in range(knots)]
        a = jnp.zeros((8, 128), F32)
        b = jnp.zeros((8, 128), F32)
        for k in range(knots):
            if k + 1 < knots:
                rise = value[k + 1] - value[k]
                a = jnp.where(row == k, value[k] - rise * float(k), a)
                b = jnp.where(row == k, rise, b)
            else:
                a = jnp.where(row == k, value[k], a)
        found += [a, b]
    return found


def kernel(
    total_depth, den, tfc, tfe, out,
    D, onehot, edge, halo_in, halo, W, A, E, tab, pb, rb, strip, bricks, blk,
    load_sem, halo_ssem, halo_rsem, strip_ssem, strip_rsem, own_sem,
    a_ssem, a_rsem, b_ssem, b_rsem, c_ssem, c_rsem,
):
    gx, gz = lax.axis_index("gx"), lax.axis_index("gz")
    n_gx, n_gz = lax.axis_size("gx"), lax.axis_size("gz")
    depth, rows, cols = den.shape
    core, chip_z, chip_x = lax.rem(gx, 2), lax.rem(gx // 2, 4), gx // 8
    NZB, NLOAD = depth // ZB, depth // ZB
    HALF = depth // 2

    def gx_of(x, z, c):
        return x * 8 + z * 2 + c

    loads = [
        pltpu.make_async_copy(
            den.at[k * ZB : (k + 1) * ZB], D.at[k * ZB : (k + 1) * ZB, RU : RU + rows, :], load_sem.at[k]
        )
        for k in range(NLOAD)
    ]
    for copy in loads:
        copy.start()

    left, right = lax.rem(gx + n_gx - 1, n_gx), lax.rem(gx + 1, n_gx)
    sibling = (gx_of(chip_x, chip_z, 1 - core), gz)
    z_peers = [(gx_of(chip_x, lax.rem(chip_z + k, 4), core), gz) for k in (1, 2, 3)]
    x_peers = [(gx_of(lax.rem(chip_x + k, 4), chip_z, core), gz) for k in (1, 2, 3)]
    y_peers = [(gx, lax.rem(gz + k, n_gz)) for k in (1, 2, 3)]
    barrier = pltpu.get_barrier_semaphore()
    peers = [(left, gz), (right, gz), sibling] + z_peers + x_peers + y_peers
    for peer in peers:
        pl.semaphore_signal(barrier, inc=1, device_id=peer, device_id_type=MESH)

    D[:, 0:RU, :] = jnp.zeros((depth, RU, cols), BF16)
    D[:, RU + rows : 2 * RU + rows, :] = jnp.zeros((depth, RU, cols), BF16)
    lane = lax.rem(iota((RU, 128), 1), HALF)

    def mark(z, _):
        onehot[z] = jnp.where(lane == z, 1.0, 0.0).astype(BF16)
        return 0

    lax.fori_loop(0, HALF, mark, 0)
    k, x = iota((cols, cols), 0), iota((cols, cols), 1)
    diff = jnp.where(k == x + 1, 1.0, 0.0) - jnp.where(k == x - 1, 1.0, 0.0)
    W[0:cols, 0:cols] = diff.astype(BF16)
    W[0:cols, cols : 2 * cols] = (0.75 * diff).astype(BF16)
    W[0:cols, 2 * cols : 3 * cols] = jnp.where(k == x, 7.0, 0.0).astype(BF16)
    k, x = iota((128, cols), 0), iota((128, cols), 1)
    diff = jnp.where((k < HALF) & (x == cols - 1), 1.0, 0.0) - jnp.where((k >= HALF) & (x == 0), 1.0, 0.0)
    W[cols : cols + 128, 0:cols] = diff.astype(BF16)
    W[cols : cols + 128, cols : 2 * cols] = (0.75 * diff).astype(BF16)
    k, x = iota((cols, 128), 0), iota((cols, 128), 1)
    E[...] = jnp.where(((k == 0) & (x < HALF)) | ((k == cols - 1) & (x >= HALF)), 1.0, 0.0).astype(BF16)
    m, k = iota((4 * RU, 12 * RU), 0), iota((4 * RU, 12 * RU), 1)
    at = (m // RU) * (3 * RU) + RU + lax.rem(m, RU)
    A[...] = (jnp.where(k == at + 1, 1.0, 0.0) - jnp.where(k == at - 1, 1.0, 0.0)).astype(BF16)
    for n, t in enumerate(tables(tfc, tfe, total_depth)):
        tab[n] = t

    lane_all = lax.rem(iota((rows, 128), 1), HALF)
    for part in range(2):
        acc = jnp.zeros((rows, 128), F32)
        for k in range(NLOAD // 2 * part, NLOAD // 2 * (part + 1)):
            loads[k].wait()
            spread = dot(D[k * ZB : (k + 1) * ZB, RU : RU + rows, :].reshape(ZB * rows, cols), E[...])
            for j in range(ZB):
                acc = jnp.where(lane_all == k * ZB + j - part * HALF, spread[j * rows : (j + 1) * rows], acc)
        edge[part] = acc.astype(BF16)

    pl.semaphore_wait(barrier, len(peers))
    halo_copies = [
        pltpu.make_async_remote_copy(
            src_ref=edge, dst_ref=halo_in.at[side], send_sem=halo_ssem.at[side], recv_sem=halo_rsem.at[side],
            device_id=(target, gz), device_id_type=MESH,
        )
        for side, target in ((0, left), (1, right))
    ]
    for copy in halo_copies:
        copy.start()
    for copy in halo_copies:
        copy.wait()
    lane_halo = iota((rows, 128), 1)
    keep_right = jnp.where(gx == n_gx - 1, 0.0, 1.0)
    keep_left = jnp.where(gx == 0, 0.0, 1.0)
    for part in range(2):
        halo[part] = jnp.where(
            lane_halo < HALF,
            halo_in[0, part].astype(F32) * keep_right,
            halo_in[1, part].astype(F32) * keep_left,
        ).astype(BF16)

    def unit_rows(u):
        return pl.multiple_of(lax.rem(gz + 1 + lax.rem(u, 4), 4) * (2 * RU) + (u // 4) * RU, RU)

    def slopes(y0, zb, pb, rb):
        z0 = pl.multiple_of(zb * ZB, ZB)
        block = D[pl.ds(z0, ZB), pl.ds(RU + y0, RU), :].reshape(ZB * RU, cols)
        part = z0 // HALF
        edges = halo[part, pl.ds(y0, RU), :][None] * onehot[pl.ds(z0 - part * HALF, ZB)]
        lhs = jnp.concatenate([block, edges.reshape(ZB * RU, 128)], 1)
        pb[0] = dot(lhs, W[:, 0:cols])
        pb[1] = dot(lhs, W[:, cols : 2 * cols])
        pb[2] = dot(block, W[0:cols, 2 * cols : 3 * cols])
        for i in range(ZB // 4):
            near = D[pl.ds(z0 + 4 * i, 4), pl.ds(y0, 3 * RU), :].reshape(12 * RU, cols)
            rb[4 * RU * i : 4 * RU * (i + 1), :] = dot(A[...], near)

    def march(y0, zb, pb, rb, carry):
        z0 = zb * ZB
        T = [tab[n] for n in range(8)]

        def step(z, carry):
            r0 = pl.multiple_of(z * RU, RU)
            dx, dx75, dens = [pb[n, pl.ds(r0, RU)] for n in range(3)]
            dy = rb[pl.ds(r0, RU)]
            new = []
            for k in range(4):
                i, j = k // 2, k % 2
                sl = (slice(8 * i, 8 * i + 8), slice(128 * j, 128 * j + 128))
                p, p75, r, d = dx[sl], dx75[sl], dy[sl], dens[sl]
                run, clear, red, green, blue = carry[5 * k : 5 * k + 5]
                q = (p75 + r) * lax.rsqrt((p * p + 0.0625) + r * r)
                ix = d.astype(jnp.int32)
                run = (run + look(T[6], ix)) + look(T[7], ix) * d
                after = jnp.exp2(run)
                w = (clear - after) * (1.25 + q)
                red = red + w * (look(T[0], ix) + look(T[1], ix) * d)
                green = green + w * (look(T[2], ix) + look(T[3], ix) * d)
                blue = blue + w * (look(T[4], ix) + look(T[5], ix) * d)
                new += [run, after, red, green, blue]
            return tuple(new)

        return lax.fori_loop(0, ZB, step, carry, unroll=True)

    def strip_copy(u):
        slot = u // 4
        target = lax.rem(gz + 1 + lax.rem(u, 4), 4)
        return pltpu.make_async_remote_copy(
            src_ref=strip.at[u], dst_ref=bricks.at[slot, gz], send_sem=strip_ssem.at[u],
            recv_sem=strip_rsem.at[slot, gz], device_id=(gx, target), device_id_type=MESH,
        )

    def column(x, z):
        return pl.multiple_of(gx_of(x, z, core) * cols, cols)

    def place(h, p, x, z):
        return out.at[2 * p : 2 * p + 2, RU * h : RU * h + RU, pl.ds(column(x, z), cols)]

    def own_copy(h):
        return pltpu.make_async_copy(
            blk.at[h], out.at[:, RU * h : RU * h + RU, pl.ds(column(chip_x, chip_z), cols)], own_sem.at[h]
        )

    def a_copies(h):
        found = []
        for p, targets, me in ((0, z_peers, chip_z), (1, x_peers, chip_x)):
            for k, target in enumerate(targets):
                found.append(
                    pltpu.make_async_remote_copy(
                        src_ref=blk.at[h, 2 * p : 2 * p + 2], dst_ref=place(h, p, chip_x, chip_z),
                        send_sem=a_ssem.at[h, p, k], recv_sem=a_rsem.at[h, p, k],
                        device_id=target, device_id_type=MESH,
                    )
                )
        return found

    def b_copy(h, p, k, n, spot):
        return pltpu.make_async_remote_copy(
            src_ref=spot, dst_ref=spot, send_sem=b_ssem.at[h, p, k, n], recv_sem=b_rsem.at[h, p, k, n],
            device_id=(x_peers, z_peers)[p][k], device_id_type=MESH,
        )

    def b_copies(h):
        return [
            b_copy(h, p, k, n, place(h, p, n, chip_z) if p else place(h, p, chip_x, n))
            for p in range(2) for k in range(3) for n in range(4)
        ]

    def a_arrivals(h):
        found = []
        for p in range(2):
            for k in range(3):
                back = 3 - k
                x = lax.rem(chip_x + back, 4) if p else chip_x
                z = chip_z if p else lax.rem(chip_z + back, 4)
                spot = place(h, p, x, z)
                found.append(
                    pltpu.make_async_remote_copy(
                        src_ref=spot, dst_ref=spot, send_sem=a_ssem.at[h, p, k], recv_sem=a_rsem.at[h, p, k],
                        device_id=(z_peers, x_peers)[p][k], device_id_type=MESH,
                    )
                )
        return found

    def b_arrivals(h):
        found = []
        for k in range(3):
            x, z = lax.rem(chip_x + 3 - k, 4), lax.rem(chip_z + 3 - k, 4)
            for n in range(4):
                found += [b_copy(h, 0, k, n, place(h, 0, x, n)), b_copy(h, 1, k, n, place(h, 1, n, z))]
        return found

    def c_copies(h, c):
        found = []
        for chip in range(16):
            at = pl.multiple_of((2 * chip + c) * cols, cols)
            spot = out.at[:, RU * h : RU * h + RU, pl.ds(at, cols)]
            found.append(
                pltpu.make_async_remote_copy(
                    src_ref=spot, dst_ref=spot, send_sem=c_ssem.at[h, chip], recv_sem=c_rsem.at[h, chip],
                    device_id=sibling, device_id_type=MESH,
                )
            )
        return found

    def composite(h):
        for k in (1, 2, 3):
            brick = lax.rem(gz + k, 4)
            pltpu.make_async_remote_copy(
                src_ref=strip.at[0], dst_ref=bricks.at[h, brick], send_sem=strip_ssem.at[0],
                recv_sem=strip_rsem.at[h, brick], device_id=(gx, brick), device_id_type=MESH,
            ).wait_recv()
        ahead = bricks[h, 0, 3]
        total = [bricks[h, 0, c] for c in range(3)] + [1.0 - ahead]
        for b in range(1, 4):
            through = bricks[h, b, 3]
            total = [total[c] + ahead * bricks[h, b, c] for c in range(3)] + [total[3] + ahead * (1.0 - through)]
            ahead = ahead * through
        for c in range(4):
            blk[h, c] = total[c].astype(BF16)
        own_copy(h).start()
        for copy in a_copies(h):
            copy.start()

    def stage_b(h):
        own_copy(h).wait()
        for copy in a_arrivals(h):
            copy.wait_recv()
        for copy in b_copies(h):
            copy.start()

    def stage_c(h):
        for copy in b_arrivals(h):
            copy.wait_recv()
        for copy in c_copies(h, core):
            copy.start()

    def unit(u, _):
        y0 = unit_rows(u)
        zero, one = jnp.zeros((8, 128), F32), jnp.ones((8, 128), F32)

        def blocks(i, carry):
            for n in range(AHEAD):
                carry = march(y0, AHEAD * i + n, pb.at[n], rb.at[n], carry)
                ahead = AHEAD * (i + 1) + n
                later = jnp.minimum(u + ahead // NZB, 4 * ROUNDS - 1)
                slopes(unit_rows(later), lax.rem(ahead, NZB), pb.at[n], rb.at[n])
            return carry

        carry = lax.fori_loop(0, NZB // AHEAD, blocks, (zero, one, zero, zero, zero) * 4)

        def keep(ref):
            for k in range(4):
                i, j = k // 2, k % 2
                _, clear, red, green, blue = carry[5 * k : 5 * k + 5]
                for c, v in enumerate((red, green, blue, clear)):
                    ref[c, 8 * i : 8 * i + 8, 128 * j : 128 * j + 128] = v

        @pl.when(lax.rem(u, 4) < 3)
        def _():
            keep(strip.at[u])
            strip_copy(u).start()

        @pl.when(lax.rem(u, 4) == 3)
        def _():
            keep(bricks.at[u // 4, gz])

        @pl.when(u == 4)
        def _():
            composite(0)

        @pl.when(u == 5)
        def _():
            stage_b(0)

        @pl.when(u == 6)
        def _():
            stage_c(0)

        return 0

    for n in range(AHEAD):
        slopes(unit_rows(0), n, pb.at[n], rb.at[n])
    lax.fori_loop(0, 4 * ROUNDS, unit, 0)
    composite(1)
    stage_b(1)
    stage_c(1)
    for h in range(ROUNDS):
        for copy in c_copies(h, 1 - core):
            copy.wait_recv()
        for copy in a_copies(h) + b_copies(h) + c_copies(h, core):
            copy.wait_send()
        for s in range(3):
            strip_copy(4 * h + s).wait_send()


def render(density, tf_color, tf_extinction):
    depth, rows, cols = density.shape
    n_gx, n_gz = lax.axis_size("gx"), lax.axis_size("gz")
    D = pltpu.SemaphoreType.DMA
    return pl.pallas_call(
        functools.partial(kernel, depth * n_gz),
        out_shape=jax.ShapeDtypeStruct((4, rows // n_gz, cols * n_gx), BF16),
        in_specs=[
            pl.BlockSpec(memory_space=pl.ANY),
            pl.BlockSpec(memory_space=pltpu.SMEM),
            pl.BlockSpec(memory_space=pltpu.SMEM),
        ],
        out_specs=pl.BlockSpec(memory_space=pl.ANY),
        scratch_shapes=[
            pltpu.VMEM((depth, rows + 2 * RU, cols), BF16),
            pltpu.VMEM((depth // 2, RU, 128), BF16),
            pltpu.VMEM((2, rows, 128), BF16),
            pltpu.VMEM((2, 2, rows, 128), BF16),
            pltpu.VMEM((2, rows, 128), BF16),
            pltpu.VMEM((cols + 128, 3 * cols), BF16),
            pltpu.VMEM((4 * RU, 12 * RU), BF16),
            pltpu.VMEM((cols, 128), BF16),
            pltpu.VMEM((8, 8, 128), F32),
            pltpu.VMEM((AHEAD, 3, ZB * RU, cols), F32),
            pltpu.VMEM((AHEAD, ZB * RU, cols), F32),
            pltpu.VMEM((4 * ROUNDS, 4, RU, cols), F32),
            pltpu.VMEM((ROUNDS, 4, 4, RU, cols), F32),
            pltpu.VMEM((ROUNDS, 4, RU, cols), BF16),
            D((depth // ZB,)),
            D((2,)),
            D((2,)),
            D((4 * ROUNDS,)),
            D((ROUNDS, 4)),
            D((ROUNDS,)),
            D((ROUNDS, 2, 3)),
            D((ROUNDS, 2, 3)),
            D((ROUNDS, 2, 3, 4)),
            D((ROUNDS, 2, 3, 4)),
            D((ROUNDS, 16)),
            D((ROUNDS, 16)),
        ],
        compiler_params=pltpu.CompilerParams(
            collective_id=0, has_side_effects=True, vmem_limit_bytes=58 * 2**20
        ),
    )(density, tf_color, tf_extinction)


def solution(mesh):
    in_specs = (P("gz", None, "gx"), P(), P())
    return jax.shard_map(
        render, mesh=mesh, in_specs=in_specs, out_specs=P(None, "gz", None), check_vma=False
    )
```

```python
import functools
import math

import jax
import jax.numpy as jnp
from jax import lax
from jax.experimental import pallas as pl
from jax.experimental.pallas import tpu as pltpu
from jax.sharding import PartitionSpec as P

F32, BF16 = jnp.float32, jnp.bfloat16
MESH = pl.DeviceIdType.MESH
RU = 16
AHEAD = 4
ZB = 8
ROUNDS = 2
UNITS = 4 * ROUNDS
GATHER = lax.GatherDimensionNumbers(
    offset_dims=(),
    collapsed_slice_dims=(0,),
    start_index_map=(0,),
    operand_batching_dims=(1,),
    start_indices_batching_dims=(1,),
)


def look(table, index):
    return lax.gather(
        table, index[..., None], GATHER, (1, 1), mode=lax.GatherScatterMode.PROMISE_IN_BOUNDS
    )


def dot(a, b):
    return jnp.dot(a, b, preferred_element_type=F32)


def iota(shape, dim):
    return lax.broadcasted_iota(jnp.int32, shape, dim)


def tables(tf, total_depth):
    knots = tf.shape[1]
    row = iota((8, 128), 0)
    found = []
    for fn in range(4):
        scale = 0.4 if fn < 3 else -math.log2(math.e) / total_depth
        value = [tf[fn, k] * scale for k in range(knots)]
        a = jnp.zeros((8, 128), F32)
        b = jnp.zeros((8, 128), F32)
        for k in range(knots):
            if k + 1 < knots:
                rise = value[k + 1] - value[k]
                a = jnp.where(row == k, value[k] - rise * float(k), a)
                b = jnp.where(row == k, rise, b)
            else:
                a = jnp.where(row == k, value[k], a)
        found += [a, b]
    return found


def kernel(
    total_depth, den, tf, out,
    D, onehot, edge, halo_in, halo, W, A, E, tab, pb, rb, strip, bricks, blk,
    load_sem, halo_ssem, halo_rsem, strip_ssem, strip_rsem, own_sem,
    a_ssem, a_rsem, b_ssem, b_rsem, c_ssem, c_rsem,
):
    gx, gz = lax.axis_index("gx"), lax.axis_index("gz")
    n_gx, n_gz = lax.axis_size("gx"), lax.axis_size("gz")
    depth, rows, cols = den.shape
    core, chip_z, chip_x = lax.rem(gx, 2), lax.rem(gx // 2, 4), gx // 8
    NZB = depth // ZB
    HALF = depth // 2

    def gx_of(x, z, c):
        return x * 8 + z * 2 + c

    def unit_rows(u):
        return pl.multiple_of(lax.rem(gz + 1 + lax.rem(u, 4), 4) * (2 * RU) + (u // 4) * RU, RU)

    def load(u):
        y0 = unit_rows(u)
        return pltpu.make_async_copy(
            den.at[:, pl.ds(y0, RU), :], D.at[:, pl.ds(RU + y0, RU), :], load_sem.at[u]
        )

    def begin_load(u, _):
        load(u).start()
        return 0

    lax.fori_loop(0, UNITS, begin_load, 0)

    left, right = lax.rem(gx + n_gx - 1, n_gx), lax.rem(gx + 1, n_gx)
    sibling = (gx_of(chip_x, chip_z, 1 - core), gz)
    z_peers = [(gx_of(chip_x, lax.rem(chip_z + k, 4), core), gz) for k in (1, 2, 3)]
    x_peers = [(gx_of(lax.rem(chip_x + k, 4), chip_z, core), gz) for k in (1, 2, 3)]
    y_peers = [(gx, lax.rem(gz + k, n_gz)) for k in (1, 2, 3)]
    barrier = pltpu.get_barrier_semaphore()
    peers = [(left, gz), (right, gz), sibling] + z_peers + x_peers + y_peers
    for peer in peers:
        pl.semaphore_signal(barrier, inc=1, device_id=peer, device_id_type=MESH)

    D[:, 0:RU, :] = jnp.zeros((depth, RU, cols), BF16)
    D[:, RU + rows : 2 * RU + rows, :] = jnp.zeros((depth, RU, cols), BF16)
    lane = lax.rem(iota((RU, 128), 1), HALF)

    def mark(z, _):
        onehot[z] = jnp.where(lane == z, 1.0, 0.0).astype(BF16)
        return 0

    lax.fori_loop(0, HALF, mark, 0)
    k, x = iota((cols, cols), 0), iota((cols, cols), 1)
    diff = jnp.where(k == x + 1, 1.0, 0.0) - jnp.where(k == x - 1, 1.0, 0.0)
    W[0:cols, 0:cols] = diff.astype(BF16)
    W[0:cols, cols : 2 * cols] = (0.75 * diff).astype(BF16)
    W[0:cols, 2 * cols : 3 * cols] = jnp.where(k == x, 7.0, 0.0).astype(BF16)
    k, x = iota((128, cols), 0), iota((128, cols), 1)
    diff = jnp.where((k < HALF) & (x == cols - 1), 1.0, 0.0) - jnp.where((k >= HALF) & (x == 0), 1.0, 0.0)
    W[cols : cols + 128, 0:cols] = diff.astype(BF16)
    W[cols : cols + 128, cols : 2 * cols] = (0.75 * diff).astype(BF16)
    k, x = iota((cols, 128), 0), iota((cols, 128), 1)
    E[...] = jnp.where(((k == 0) & (x < HALF)) | ((k == cols - 1) & (x >= HALF)), 1.0, 0.0).astype(BF16)
    m, k = iota((4 * RU, 12 * RU), 0), iota((4 * RU, 12 * RU), 1)
    at = (m // RU) * (3 * RU) + RU + lax.rem(m, RU)
    A[...] = (jnp.where(k == at + 1, 1.0, 0.0) - jnp.where(k == at - 1, 1.0, 0.0)).astype(BF16)
    for n, t in enumerate(tables(tf, total_depth)):
        tab[n] = t

    lane_half = lax.rem(iota((RU, 128), 1), HALF)
    lane_halo = iota((RU, 128), 1)
    keep_right = jnp.where(gx == n_gx - 1, 0.0, 1.0)
    keep_left = jnp.where(gx == 0, 0.0, 1.0)

    def extract(u):
        load(u).wait()
        y0 = unit_rows(u)
        for part in range(2):
            block = D[part * HALF : (part + 1) * HALF, pl.ds(RU + y0, RU), :].reshape(HALF * RU, cols)
            spread = dot(block, E[...])
            acc = jnp.zeros((RU, 128), F32)
            for z in range(HALF):
                acc = jnp.where(lane_half == z, spread[z * RU : (z + 1) * RU], acc)
            edge[u, part] = acc.astype(BF16)

    def halo_copies(u):
        return [
            pltpu.make_async_remote_copy(
                src_ref=edge.at[u], dst_ref=halo_in.at[side, u], send_sem=halo_ssem.at[side, u],
                recv_sem=halo_rsem.at[side, u], device_id=(target, gz), device_id_type=MESH,
            )
            for side, target in ((0, left), (1, right))
        ]

    def halo_arrive(u):
        for copy in halo_copies(u):
            copy.wait()
        for part in range(2):
            halo[u, part] = jnp.where(
                lane_halo < HALF,
                halo_in[0, u, part].astype(F32) * keep_right,
                halo_in[1, u, part].astype(F32) * keep_left,
            ).astype(BF16)

    extract(0)
    pl.semaphore_wait(barrier, len(peers))
    for copy in halo_copies(0):
        copy.start()

    def send_edges(u, _):
        extract(u)
        for copy in halo_copies(u):
            copy.start()
        return 0

    lax.fori_loop(1, UNITS, send_edges, 0)
    halo_arrive(0)

    def slopes(u, zb, pb, rb):
        y0 = unit_rows(u)
        z0 = pl.multiple_of(zb * ZB, ZB)
        block = D[pl.ds(z0, ZB), pl.ds(RU + y0, RU), :].reshape(ZB * RU, cols)
        part = z0 // HALF
        edges = halo[u, part][None] * onehot[pl.ds(z0 - part * HALF, ZB)]
        lhs = jnp.concatenate([block, edges.reshape(ZB * RU, 128)], 1)
        pb[0] = dot(lhs, W[:, 0:cols])
        pb[1] = dot(lhs, W[:, cols : 2 * cols])
        pb[2] = dot(block, W[0:cols, 2 * cols : 3 * cols])
        for i in range(ZB // 4):
            near = D[pl.ds(z0 + 4 * i, 4), pl.ds(y0, 3 * RU), :].reshape(12 * RU, cols)
            rb[4 * RU * i : 4 * RU * (i + 1), :] = dot(A[...], near)

    def march(y0, zb, pb, rb, carry):
        z0 = zb * ZB
        T = [tab[n] for n in range(8)]

        def step(z, carry):
            r0 = pl.multiple_of(z * RU, RU)
            dx, dx75, dens = [pb[n, pl.ds(r0, RU)] for n in range(3)]
            dy = rb[pl.ds(r0, RU)]
            new = []
            for k in range(4):
                i, j = k // 2, k % 2
                sl = (slice(8 * i, 8 * i + 8), slice(128 * j, 128 * j + 128))
                p, p75, r, d = dx[sl], dx75[sl], dy[sl], dens[sl]
                run, clear, red, green, blue = carry[5 * k : 5 * k + 5]
                q = (p75 + r) * lax.rsqrt((p * p + 0.0625) + r * r)
                ix = d.astype(jnp.int32)
                run = (run + look(T[6], ix)) + look(T[7], ix) * d
                after = jnp.exp2(run)
                w = (clear - after) * (1.25 + q)
                red = red + w * (look(T[0], ix) + look(T[1], ix) * d)
                green = green + w * (look(T[2], ix) + look(T[3], ix) * d)
                blue = blue + w * (look(T[4], ix) + look(T[5], ix) * d)
                new += [run, after, red, green, blue]
            return tuple(new)

        return lax.fori_loop(0, ZB, step, carry, unroll=True)

    def strip_copy(u):
        slot = u // 4
        target = lax.rem(gz + 1 + lax.rem(u, 4), 4)
        return pltpu.make_async_remote_copy(
            src_ref=strip.at[u], dst_ref=bricks.at[slot, gz], send_sem=strip_ssem.at[u],
            recv_sem=strip_rsem.at[slot, gz], device_id=(gx, target), device_id_type=MESH,
        )

    first, second = (z_peers, x_peers), (x_peers, z_peers)

    def place(h, p, k, j, c):
        x, z = lax.rem(chip_x + (j if p else k), 4), lax.rem(chip_z + (k if p else j), 4)
        at = pl.multiple_of(gx_of(x, z, c) * cols, cols)
        return out.at[2 * p : 2 * p + 2, RU * h : RU * h + RU, pl.ds(at, cols)]

    def own_copy(h):
        at = pl.multiple_of(gx * cols, cols)
        return pltpu.make_async_copy(blk.at[h], out.at[:, RU * h : RU * h + RU, pl.ds(at, cols)], own_sem.at[h])

    def held(h, p, k, j):
        return blk.at[h, 2 * p : 2 * p + 2] if k == 0 and j == 0 else place(h, p, k, j, core)

    def send(src, dst, ssem, rsem, target):
        return pltpu.make_async_remote_copy(
            src_ref=src, dst_ref=dst, send_sem=ssem, recv_sem=rsem, device_id=target, device_id_type=MESH
        )

    def a_copy(h, p, m):
        return send(held(h, p, 0, 0), place(h, p, 0, 0, core), a_ssem.at[h, p, m - 1], a_rsem.at[h, p, m - 1], first[p][m - 1])

    def a_arrival(h, p, j):
        spot = place(h, p, 0, j, core)
        return send(spot, spot, a_ssem.at[h, p, 3 - j], a_rsem.at[h, p, 3 - j], first[p][3 - j])

    def b_copy(h, p, m, j):
        return send(held(h, p, 0, j), place(h, p, 0, j, core), b_ssem.at[h, p, m - 1, j], b_rsem.at[h, p, m - 1, j], second[p][m - 1])

    def b_arrival(h, p, k, j):
        spot = place(h, p, k, j, core)
        return send(spot, spot, b_ssem.at[h, p, 3 - k, j], b_rsem.at[h, p, 3 - k, j], second[p][3 - k])

    def c_copy(h, p, k, j):
        return send(held(h, p, k, j), place(h, p, k, j, core), c_ssem.at[h, p, k, j], c_rsem.at[h, p, k, j], sibling)

    def c_arrival(h, p, k, j):
        spot = place(h, p, k, j, 1 - core)
        return send(spot, spot, c_ssem.at[h, p, k, j], c_rsem.at[h, p, k, j], sibling)

    NEAR = (1, 3, 2)

    def composite(h):
        for k in (1, 2, 3):
            brick = lax.rem(gz + k, 4)
            pltpu.make_async_remote_copy(
                src_ref=strip.at[0], dst_ref=bricks.at[h, brick], send_sem=strip_ssem.at[0],
                recv_sem=strip_rsem.at[h, brick], device_id=(gx, brick), device_id_type=MESH,
            ).wait_recv()
        ahead = bricks[h, 0, 3]
        total = [bricks[h, 0, c] for c in range(3)] + [1.0 - ahead]
        for b in range(1, 4):
            through = bricks[h, b, 3]
            total = [total[c] + ahead * bricks[h, b, c] for c in range(3)] + [total[3] + ahead * (1.0 - through)]
            ahead = ahead * through
        for c in range(4):
            blk[h, c] = total[c].astype(BF16)
        for p in range(2):
            for m in NEAR:
                a_copy(h, p, m).start()
        for p in range(2):
            for m in NEAR:
                b_copy(h, p, m, 0).start()
        own_copy(h).start()
        for p in range(2):
            c_copy(h, p, 0, 0).start()

    def stage_b(h):
        own_copy(h).wait()
        for j in NEAR:
            for p in range(2):
                a_arrival(h, p, j).wait_recv()
                for m in NEAR:
                    b_copy(h, p, m, j).start()
                c_copy(h, p, 0, j).start()

    def stage_c(h):
        for j in (0,) + NEAR:
            for k in NEAR:
                for p in range(2):
                    b_arrival(h, p, k, j).wait_recv()
                    c_copy(h, p, k, j).start()

    def unit(u, _):
        y0 = unit_rows(u)
        zero, one = jnp.zeros((8, 128), F32), jnp.ones((8, 128), F32)

        def blocks(i, carry):
            @pl.when((i == NZB // AHEAD - 2) & (u < UNITS - 1))
            def _():
                halo_arrive(u + 1)

            for n in range(AHEAD):
                carry = march(y0, AHEAD * i + n, pb.at[n], rb.at[n], carry)
                ahead = AHEAD * (i + 1) + n
                later = jnp.minimum(u + ahead // NZB, UNITS - 1)
                slopes(later, lax.rem(ahead, NZB), pb.at[n], rb.at[n])
            return carry

        carry = lax.fori_loop(0, NZB // AHEAD, blocks, (zero, one, zero, zero, zero) * 4)

        def keep(ref):
            for k in range(4):
                i, j = k // 2, k % 2
                _, clear, red, green, blue = carry[5 * k : 5 * k + 5]
                for c, v in enumerate((red, green, blue, clear)):
                    ref[c, 8 * i : 8 * i + 8, 128 * j : 128 * j + 128] = v

        @pl.when(lax.rem(u, 4) < 3)
        def _():
            keep(strip.at[u])
            strip_copy(u).start()

        @pl.when(lax.rem(u, 4) == 3)
        def _():
            keep(bricks.at[u // 4, gz])

        @pl.when(u == 4)
        def _():
            composite(0)

        @pl.when(u == 5)
        def _():
            stage_b(0)

        @pl.when(u == 6)
        def _():
            stage_c(0)

        return 0

    for n in range(AHEAD):
        slopes(0, n, pb.at[n], rb.at[n])
    lax.fori_loop(0, UNITS, unit, 0)
    composite(1)
    stage_b(1)
    stage_c(1)
    for h in range(ROUNDS):
        for p in range(2):
            for j in range(4):
                for k in range(4):
                    c_arrival(h, p, k, j).wait_recv()
                    c_copy(h, p, k, j).wait_send()
                    if k:
                        b_copy(h, p, k, j).wait_send()
                if j:
                    a_copy(h, p, j).wait_send()
        for i in range(3):
            strip_copy(4 * h + i).wait_send()


def render(density, tf_color, tf_extinction):
    depth, rows, cols = density.shape
    n_gx, n_gz = lax.axis_size("gx"), lax.axis_size("gz")
    D = pltpu.SemaphoreType.DMA
    return pl.pallas_call(
        functools.partial(kernel, depth * n_gz),
        out_shape=jax.ShapeDtypeStruct((4, rows // n_gz, cols * n_gx), BF16),
        in_specs=[
            pl.BlockSpec(memory_space=pl.ANY),
            pl.BlockSpec(memory_space=pltpu.SMEM),
        ],
        out_specs=pl.BlockSpec(memory_space=pl.ANY),
        scratch_shapes=[
            pltpu.VMEM((depth, rows + 2 * RU, cols), BF16),
            pltpu.VMEM((depth // 2, RU, 128), BF16),
            pltpu.VMEM((UNITS, 2, RU, 128), BF16),
            pltpu.VMEM((2, UNITS, 2, RU, 128), BF16),
            pltpu.VMEM((UNITS, 2, RU, 128), BF16),
            pltpu.VMEM((cols + 128, 3 * cols), BF16),
            pltpu.VMEM((4 * RU, 12 * RU), BF16),
            pltpu.VMEM((cols, 128), BF16),
            pltpu.VMEM((8, 8, 128), F32),
            pltpu.VMEM((AHEAD, 3, ZB * RU, cols), F32),
            pltpu.VMEM((AHEAD, ZB * RU, cols), F32),
            pltpu.VMEM((4 * ROUNDS, 4, RU, cols), F32),
            pltpu.VMEM((ROUNDS, 4, 4, RU, cols), F32),
            pltpu.VMEM((ROUNDS, 4, RU, cols), BF16),
            D((UNITS,)),
            D((2, UNITS)),
            D((2, UNITS)),
            D((UNITS,)),
            D((ROUNDS, 4)),
            D((ROUNDS,)),
            D((ROUNDS, 2, 3)),
            D((ROUNDS, 2, 3)),
            D((ROUNDS, 2, 3, 4)),
            D((ROUNDS, 2, 3, 4)),
            D((ROUNDS, 2, 4, 4)),
            D((ROUNDS, 2, 4, 4)),
        ],
        compiler_params=pltpu.CompilerParams(
            collective_id=0, has_side_effects=True, vmem_limit_bytes=50 * 2**20
        ),
    )(density, jnp.concatenate([tf_color, tf_extinction[None]], 0))


def solution(mesh):
    in_specs = (P("gz", None, "gx"), P(), P())
    return jax.shard_map(
        render, mesh=mesh, in_specs=in_specs, out_specs=P(None, "gz", None), check_vma=False
    )
```

```python
import functools
import math

import jax
import jax.numpy as jnp
from jax import lax
from jax.experimental import pallas as pl
from jax.experimental.pallas import tpu as pltpu
from jax.sharding import PartitionSpec as P

F32, BF16 = jnp.float32, jnp.bfloat16
MESH = pl.DeviceIdType.MESH
RU = 16
AHEAD = 8
ZB = 8
ROUNDS = 2
UNITS = 4 * ROUNDS
GATHER = lax.GatherDimensionNumbers(
    offset_dims=(),
    collapsed_slice_dims=(0,),
    start_index_map=(0,),
    operand_batching_dims=(1,),
    start_indices_batching_dims=(1,),
)


def look(table, index):
    return lax.gather(
        table, index[..., None], GATHER, (1, 1), mode=lax.GatherScatterMode.PROMISE_IN_BOUNDS
    )


def dot(a, b):
    return jnp.dot(a, b, preferred_element_type=F32)


def iota(shape, dim):
    return lax.broadcasted_iota(jnp.int32, shape, dim)


def tables(tf, total_depth):
    knots = tf.shape[1]
    row = iota((8, 128), 0)
    found = []
    for fn in range(4):
        scale = 0.4 if fn < 3 else -math.log2(math.e) / total_depth
        value = [tf[fn, k] * scale for k in range(knots)]
        a = jnp.zeros((8, 128), F32)
        b = jnp.zeros((8, 128), F32)
        for k in range(knots):
            if k + 1 < knots:
                rise = value[k + 1] - value[k]
                a = jnp.where(row == k, value[k] - rise * float(k), a)
                b = jnp.where(row == k, rise, b)
            else:
                a = jnp.where(row == k, value[k], a)
        found += [a, b]
    return found


def kernel(
    total_depth, den, tf, out,
    D, onehot, edge, halo_in, halo, W, A, E, tab, pb, rb, strip, bricks, blk,
    load_sem, halo_ssem, halo_rsem, strip_ssem, strip_rsem, own_sem,
    a_ssem, a_rsem, b_ssem, b_rsem, c_ssem, c_rsem,
):
    gx, gz = lax.axis_index("gx"), lax.axis_index("gz")
    n_gx, n_gz = lax.axis_size("gx"), lax.axis_size("gz")
    depth, rows, cols = den.shape
    core, chip_z, chip_x = lax.rem(gx, 2), lax.rem(gx // 2, 4), gx // 8
    NZB = depth // ZB
    HALF = depth // 2

    def gx_of(x, z, c):
        return x * 8 + z * 2 + c

    def unit_rows(u):
        return pl.multiple_of(lax.rem(gz + 1 + lax.rem(u, 4), 4) * (2 * RU) + (u // 4) * RU, RU)

    def load(u):
        y0 = unit_rows(u)
        return pltpu.make_async_copy(
            den.at[:, pl.ds(y0, RU), :], D.at[:, pl.ds(RU + y0, RU), :], load_sem.at[u]
        )

    def begin_load(u, _):
        load(u).start()
        return 0

    lax.fori_loop(0, UNITS, begin_load, 0)

    left, right = lax.rem(gx + n_gx - 1, n_gx), lax.rem(gx + 1, n_gx)
    sibling = (gx_of(chip_x, chip_z, 1 - core), gz)
    z_peers = [(gx_of(chip_x, lax.rem(chip_z + k, 4), core), gz) for k in (1, 2, 3)]
    x_peers = [(gx_of(lax.rem(chip_x + k, 4), chip_z, core), gz) for k in (1, 2, 3)]
    y_peers = [(gx, lax.rem(gz + k, n_gz)) for k in (1, 2, 3)]
    barrier = pltpu.get_barrier_semaphore()
    peers = [(left, gz), (right, gz), sibling] + z_peers + x_peers + y_peers
    for peer in peers:
        pl.semaphore_signal(barrier, inc=1, device_id=peer, device_id_type=MESH)

    D[:, 0:RU, :] = jnp.zeros((depth, RU, cols), BF16)
    D[:, RU + rows : 2 * RU + rows, :] = jnp.zeros((depth, RU, cols), BF16)
    lane = lax.rem(iota((RU, 128), 1), HALF)

    def mark(z, _):
        onehot[z] = jnp.where(lane == z, 1.0, 0.0).astype(BF16)
        return 0

    lax.fori_loop(0, HALF, mark, 0)
    k, x = iota((cols, cols), 0), iota((cols, cols), 1)
    diff = jnp.where(k == x + 1, 1.0, 0.0) - jnp.where(k == x - 1, 1.0, 0.0)
    W[0:cols, 0:cols] = diff.astype(BF16)
    W[0:cols, cols : 2 * cols] = jnp.where(k == x, 7.0, 0.0).astype(BF16)
    k, x = iota((128, cols), 0), iota((128, cols), 1)
    diff = jnp.where((k < HALF) & (x == cols - 1), 1.0, 0.0) - jnp.where((k >= HALF) & (x == 0), 1.0, 0.0)
    W[cols : cols + 128, 0:cols] = diff.astype(BF16)
    k, x = iota((cols, 128), 0), iota((cols, 128), 1)
    E[...] = jnp.where(((k == 0) & (x < HALF)) | ((k == cols - 1) & (x >= HALF)), 1.0, 0.0).astype(BF16)
    m, k = iota((4 * RU, 12 * RU), 0), iota((4 * RU, 12 * RU), 1)
    at = (m // RU) * (3 * RU) + RU + lax.rem(m, RU)
    A[...] = (jnp.where(k == at + 1, 1.0, 0.0) - jnp.where(k == at - 1, 1.0, 0.0)).astype(BF16)
    for n, t in enumerate(tables(tf, total_depth)):
        tab[n] = t

    lane_half = lax.rem(iota((RU, 128), 1), HALF)
    lane_halo = iota((RU, 128), 1)
    keep_right = jnp.where(gx == n_gx - 1, 0.0, 1.0)
    keep_left = jnp.where(gx == 0, 0.0, 1.0)

    def extract(u):
        load(u).wait()
        y0 = unit_rows(u)
        for part in range(2):
            block = D[part * HALF : (part + 1) * HALF, pl.ds(RU + y0, RU), :].reshape(HALF * RU, cols)
            spread = dot(block, E[...])
            acc = jnp.zeros((RU, 128), F32)
            for z in range(HALF):
                acc = jnp.where(lane_half == z, spread[z * RU : (z + 1) * RU], acc)
            edge[u, part] = acc.astype(BF16)

    def halo_copies(u):
        return [
            pltpu.make_async_remote_copy(
                src_ref=edge.at[u], dst_ref=halo_in.at[side, u], send_sem=halo_ssem.at[side, u],
                recv_sem=halo_rsem.at[side, u], device_id=(target, gz), device_id_type=MESH,
            )
            for side, target in ((0, left), (1, right))
        ]

    def halo_arrive(u):
        for copy in halo_copies(u):
            copy.wait()
        for part in range(2):
            halo[u, part] = jnp.where(
                lane_halo < HALF,
                halo_in[0, u, part].astype(F32) * keep_right,
                halo_in[1, u, part].astype(F32) * keep_left,
            ).astype(BF16)

    extract(0)
    pl.semaphore_wait(barrier, len(peers))
    for copy in halo_copies(0):
        copy.start()

    def send_edges(u, _):
        extract(u)
        for copy in halo_copies(u):
            copy.start()
        return 0

    lax.fori_loop(1, UNITS, send_edges, 0)
    halo_arrive(0)

    def slopes(u, zb, pb, rb):
        y0 = unit_rows(u)
        z0 = pl.multiple_of(zb * ZB, ZB)
        block = D[pl.ds(z0, ZB), pl.ds(RU + y0, RU), :].reshape(ZB * RU, cols)
        part = z0 // HALF
        edges = halo[u, part][None] * onehot[pl.ds(z0 - part * HALF, ZB)]
        lhs = jnp.concatenate([block, edges.reshape(ZB * RU, 128)], 1)
        pb[0] = dot(lhs, W[:, 0:cols])
        pb[1] = dot(block, W[0:cols, cols : 2 * cols])
        for i in range(ZB // 4):
            near = D[pl.ds(z0 + 4 * i, 4), pl.ds(y0, 3 * RU), :].reshape(12 * RU, cols)
            rb[4 * RU * i : 4 * RU * (i + 1), :] = dot(A[...], near)

    def march(y0, zb, pb, rb, carry):
        z0 = zb * ZB
        T = [tab[n] for n in range(8)]

        def step(z, carry):
            r0 = pl.multiple_of(z * RU, RU)
            dx, dens = [pb[n, pl.ds(r0, RU)] for n in range(2)]
            dy = rb[pl.ds(r0, RU)]
            new = []
            for k in range(4):
                i, j = k // 2, k % 2
                sl = (slice(8 * i, 8 * i + 8), slice(128 * j, 128 * j + 128))
                p, r, d = dx[sl], dy[sl], dens[sl]
                run, clear, red, green, blue = carry[5 * k : 5 * k + 5]
                q = (0.75 * p + r) * lax.rsqrt((p * p + 0.0625) + r * r)
                ix = d.astype(jnp.int32)
                run = (run + look(T[6], ix)) + look(T[7], ix) * d
                after = jnp.exp2(run)
                w = (clear - after) * (1.25 + q)
                red = red + w * (look(T[0], ix) + look(T[1], ix) * d)
                green = green + w * (look(T[2], ix) + look(T[3], ix) * d)
                blue = blue + w * (look(T[4], ix) + look(T[5], ix) * d)
                new += [run, after, red, green, blue]
            return tuple(new)

        return lax.fori_loop(0, ZB, step, carry, unroll=True)

    def strip_copy(u):
        slot = u // 4
        target = lax.rem(gz + 1 + lax.rem(u, 4), 4)
        return pltpu.make_async_remote_copy(
            src_ref=strip.at[u], dst_ref=bricks.at[slot, gz], send_sem=strip_ssem.at[u],
            recv_sem=strip_rsem.at[slot, gz], device_id=(gx, target), device_id_type=MESH,
        )

    first, second = (z_peers, x_peers), (x_peers, z_peers)

    def place(h, p, k, j, c):
        x, z = lax.rem(chip_x + (j if p else k), 4), lax.rem(chip_z + (k if p else j), 4)
        at = pl.multiple_of(gx_of(x, z, c) * cols, cols)
        return out.at[2 * p : 2 * p + 2, RU * h : RU * h + RU, pl.ds(at, cols)]

    def own_copy(h):
        at = pl.multiple_of(gx * cols, cols)
        return pltpu.make_async_copy(blk.at[h], out.at[:, RU * h : RU * h + RU, pl.ds(at, cols)], own_sem.at[h])

    def held(h, p, k, j):
        return blk.at[h, 2 * p : 2 * p + 2] if k == 0 and j == 0 else place(h, p, k, j, core)

    def send(src, dst, ssem, rsem, target):
        return pltpu.make_async_remote_copy(
            src_ref=src, dst_ref=dst, send_sem=ssem, recv_sem=rsem, device_id=target, device_id_type=MESH
        )

    def a_copy(h, p, m):
        return send(held(h, p, 0, 0), place(h, p, 0, 0, core), a_ssem.at[h, p, m - 1], a_rsem.at[h, p, m - 1], first[p][m - 1])

    def a_arrival(h, p, j):
        spot = place(h, p, 0, j, core)
        return send(spot, spot, a_ssem.at[h, p, 3 - j], a_rsem.at[h, p, 3 - j], first[p][3 - j])

    def b_copy(h, p, m, j):
        return send(held(h, p, 0, j), place(h, p, 0, j, core), b_ssem.at[h, p, m - 1, j], b_rsem.at[h, p, m - 1, j], second[p][m - 1])

    def b_arrival(h, p, k, j):
        spot = place(h, p, k, j, core)
        return send(spot, spot, b_ssem.at[h, p, 3 - k, j], b_rsem.at[h, p, 3 - k, j], second[p][3 - k])

    def c_copy(h, p, k, j):
        return send(held(h, p, k, j), place(h, p, k, j, core), c_ssem.at[h, p, k, j], c_rsem.at[h, p, k, j], sibling)

    def c_arrival(h, p, k, j):
        spot = place(h, p, k, j, 1 - core)
        return send(spot, spot, c_ssem.at[h, p, k, j], c_rsem.at[h, p, k, j], sibling)

    NEAR = (1, 3, 2)

    def composite(h):
        for k in (1, 2, 3):
            brick = lax.rem(gz + k, 4)
            pltpu.make_async_remote_copy(
                src_ref=strip.at[0], dst_ref=bricks.at[h, brick], send_sem=strip_ssem.at[0],
                recv_sem=strip_rsem.at[h, brick], device_id=(gx, brick), device_id_type=MESH,
            ).wait_recv()
        ahead = bricks[h, 0, 3]
        total = [bricks[h, 0, c] for c in range(3)] + [1.0 - ahead]
        for b in range(1, 4):
            through = bricks[h, b, 3]
            total = [total[c] + ahead * bricks[h, b, c] for c in range(3)] + [total[3] + ahead * (1.0 - through)]
            ahead = ahead * through
        for c in range(4):
            blk[h, c] = total[c].astype(BF16)
        for p in range(2):
            for m in NEAR:
                a_copy(h, p, m).start()
        for p in range(2):
            for m in NEAR:
                b_copy(h, p, m, 0).start()
        own_copy(h).start()
        for p in range(2):
            c_copy(h, p, 0, 0).start()

    def stage_b(h):
        own_copy(h).wait()
        for j in NEAR:
            for p in range(2):
                a_arrival(h, p, j).wait_recv()
                for m in NEAR:
                    b_copy(h, p, m, j).start()
                c_copy(h, p, 0, j).start()

    def stage_c(h):
        for j in (0,) + NEAR:
            for k in NEAR:
                for p in range(2):
                    b_arrival(h, p, k, j).wait_recv()
                    c_copy(h, p, k, j).start()

    def unit(u, _):
        y0 = unit_rows(u)
        zero, one = jnp.zeros((8, 128), F32), jnp.ones((8, 128), F32)

        def blocks(i, carry):
            @pl.when((i == NZB // AHEAD - 2) & (u < UNITS - 1))
            def _():
                halo_arrive(u + 1)

            for n in range(AHEAD):
                carry = march(y0, AHEAD * i + n, pb.at[n], rb.at[n], carry)
                ahead = AHEAD * (i + 1) + n
                later = jnp.minimum(u + ahead // NZB, UNITS - 1)
                slopes(later, lax.rem(ahead, NZB), pb.at[n], rb.at[n])
            return carry

        carry = lax.fori_loop(0, NZB // AHEAD, blocks, (zero, one, zero, zero, zero) * 4)

        def keep(ref):
            for k in range(4):
                i, j = k // 2, k % 2
                _, clear, red, green, blue = carry[5 * k : 5 * k + 5]
                for c, v in enumerate((red, green, blue, clear)):
                    ref[c, 8 * i : 8 * i + 8, 128 * j : 128 * j + 128] = v

        @pl.when(lax.rem(u, 4) < 3)
        def _():
            keep(strip.at[u])
            strip_copy(u).start()

        @pl.when(lax.rem(u, 4) == 3)
        def _():
            keep(bricks.at[u // 4, gz])

        @pl.when(u == 4)
        def _():
            composite(0)

        @pl.when(u == 5)
        def _():
            stage_b(0)

        @pl.when(u == 6)
        def _():
            stage_c(0)

        return 0

    for n in range(AHEAD):
        slopes(0, n, pb.at[n], rb.at[n])
    lax.fori_loop(0, UNITS, unit, 0)
    def finish(h):
        for p in range(2):
            for j in range(4):
                for k in range(4):
                    c_arrival(h, p, k, j).wait_recv()
                    c_copy(h, p, k, j).wait_send()

    def sent(h):
        for p in range(2):
            for m in range(1, 4):
                for j in range(4):
                    b_copy(h, p, m, j).wait_send()
                a_copy(h, p, m).wait_send()
        for i in range(3):
            strip_copy(4 * h + i).wait_send()

    composite(1)
    finish(0)
    stage_b(1)
    sent(0)
    stage_c(1)
    sent(1)
    finish(1)


def render(density, tf_color, tf_extinction):
    depth, rows, cols = density.shape
    n_gx, n_gz = lax.axis_size("gx"), lax.axis_size("gz")
    D = pltpu.SemaphoreType.DMA
    return pl.pallas_call(
        functools.partial(kernel, depth * n_gz),
        out_shape=jax.ShapeDtypeStruct((4, rows // n_gz, cols * n_gx), BF16),
        in_specs=[
            pl.BlockSpec(memory_space=pl.ANY),
            pl.BlockSpec(memory_space=pltpu.SMEM),
        ],
        out_specs=pl.BlockSpec(memory_space=pl.ANY),
        scratch_shapes=[
            pltpu.VMEM((depth, rows + 2 * RU, cols), BF16),
            pltpu.VMEM((depth // 2, RU, 128), BF16),
            pltpu.VMEM((UNITS, 2, RU, 128), BF16),
            pltpu.VMEM((2, UNITS, 2, RU, 128), BF16),
            pltpu.VMEM((UNITS, 2, RU, 128), BF16),
            pltpu.VMEM((cols + 128, 2 * cols), BF16),
            pltpu.VMEM((4 * RU, 12 * RU), BF16),
            pltpu.VMEM((cols, 128), BF16),
            pltpu.VMEM((8, 8, 128), F32),
            pltpu.VMEM((AHEAD, 2, ZB * RU, cols), F32),
            pltpu.VMEM((AHEAD, ZB * RU, cols), F32),
            pltpu.VMEM((4 * ROUNDS, 4, RU, cols), F32),
            pltpu.VMEM((ROUNDS, 4, 4, RU, cols), F32),
            pltpu.VMEM((ROUNDS, 4, RU, cols), BF16),
            D((UNITS,)),
            D((2, UNITS)),
            D((2, UNITS)),
            D((UNITS,)),
            D((ROUNDS, 4)),
            D((ROUNDS,)),
            D((ROUNDS, 2, 3)),
            D((ROUNDS, 2, 3)),
            D((ROUNDS, 2, 3, 4)),
            D((ROUNDS, 2, 3, 4)),
            D((ROUNDS, 2, 4, 4)),
            D((ROUNDS, 2, 4, 4)),
        ],
        compiler_params=pltpu.CompilerParams(
            collective_id=0, has_side_effects=True, vmem_limit_bytes=50 * 2**20
        ),
    )(density, jnp.concatenate([tf_color, tf_extinction[None]], 0))


def solution(mesh):
    in_specs = (P("gz", None, "gx"), P(), P())
    return jax.shard_map(
        render, mesh=mesh, in_specs=in_specs, out_specs=P(None, "gz", None), check_vma=False
    )
```

```python
import functools
import math

import jax
import jax.numpy as jnp
from jax import lax
from jax.experimental import pallas as pl
from jax.experimental.pallas import tpu as pltpu
from jax.sharding import PartitionSpec as P

F32, BF16 = jnp.float32, jnp.bfloat16
MESH = pl.DeviceIdType.MESH
RU = 16
AHEAD = 8
ZB = 8
ROUNDS = 2
UNITS = 4 * ROUNDS
GATHER = lax.GatherDimensionNumbers(
    offset_dims=(),
    collapsed_slice_dims=(0,),
    start_index_map=(0,),
    operand_batching_dims=(1,),
    start_indices_batching_dims=(1,),
)


def look(table, index):
    return lax.gather(
        table, index[..., None], GATHER, (1, 1), mode=lax.GatherScatterMode.PROMISE_IN_BOUNDS
    )


def dot(a, b):
    return jnp.dot(a, b, preferred_element_type=F32)


def iota(shape, dim):
    return lax.broadcasted_iota(jnp.int32, shape, dim)


def tables(tf, total_depth):
    knots = tf.shape[1]
    row = iota((8, 128), 0)
    found = []
    for fn in range(4):
        scale = 0.4 if fn < 3 else -math.log2(math.e) / total_depth
        value = [tf[fn, k] * scale for k in range(knots)]
        a = jnp.zeros((8, 128), F32)
        b = jnp.zeros((8, 128), F32)
        for k in range(knots):
            if k + 1 < knots:
                rise = value[k + 1] - value[k]
                a = jnp.where(row == k, value[k] - rise * float(k), a)
                b = jnp.where(row == k, rise, b)
            else:
                a = jnp.where(row == k, value[k], a)
        found += [a, b]
    return found


def kernel(
    total_depth, den, tf, out,
    D, onehot, edge, halo_in, halo, W, A, E, tab, pb, rb, strip, bricks, blk,
    load_sem, halo_ssem, halo_rsem, strip_ssem, strip_rsem, own_sem,
    a_ssem, a_rsem, b_ssem, b_rsem, c_ssem, c_rsem,
):
    gx, gz = lax.axis_index("gx"), lax.axis_index("gz")
    n_gx, n_gz = lax.axis_size("gx"), lax.axis_size("gz")
    depth, rows, cols = den.shape
    core, chip_z, chip_x = lax.rem(gx, 2), lax.rem(gx // 2, 4), gx // 8
    NZB = depth // ZB
    HALF = depth // 2

    def gx_of(x, z, c):
        return x * 8 + z * 2 + c

    def unit_rows(u):
        return pl.multiple_of(lax.rem(gz + 1 + lax.rem(u, 4), 4) * (2 * RU) + (u // 4) * RU, RU)

    def load(u):
        y0 = unit_rows(u)
        return pltpu.make_async_copy(
            den.at[:, pl.ds(y0, RU), :], D.at[:, pl.ds(RU + y0, RU), :], load_sem.at[u]
        )

    def begin_load(u, _):
        load(u).start()
        return 0

    lax.fori_loop(0, UNITS, begin_load, 0)

    left, right = lax.rem(gx + n_gx - 1, n_gx), lax.rem(gx + 1, n_gx)
    sibling = (gx_of(chip_x, chip_z, 1 - core), gz)
    z_peers = [(gx_of(chip_x, lax.rem(chip_z + k, 4), core), gz) for k in (1, 2, 3)]
    x_peers = [(gx_of(lax.rem(chip_x + k, 4), chip_z, core), gz) for k in (1, 2, 3)]
    y_peers = [(gx, lax.rem(gz + k, n_gz)) for k in (1, 2, 3)]
    barrier = pltpu.get_barrier_semaphore()
    peers = [(left, gz), (right, gz), sibling] + z_peers + x_peers + y_peers
    for peer in peers:
        pl.semaphore_signal(barrier, inc=1, device_id=peer, device_id_type=MESH)

    D[:, 0:RU, :] = jnp.zeros((depth, RU, cols), BF16)
    D[:, RU + rows : 2 * RU + rows, :] = jnp.zeros((depth, RU, cols), BF16)
    lane = lax.rem(iota((RU, 128), 1), HALF)

    def mark(z, _):
        onehot[z] = jnp.where(lane == z, 1.0, 0.0).astype(BF16)
        return 0

    lax.fori_loop(0, HALF, mark, 0)
    k, x = iota((cols, cols), 0), iota((cols, cols), 1)
    diff = jnp.where(k == x + 1, 1.0, 0.0) - jnp.where(k == x - 1, 1.0, 0.0)
    W[0:cols, 0:cols] = diff.astype(BF16)
    W[0:cols, cols : 2 * cols] = jnp.where(k == x, 7.0, 0.0).astype(BF16)
    k, x = iota((128, cols), 0), iota((128, cols), 1)
    diff = jnp.where((k < HALF) & (x == cols - 1), 1.0, 0.0) - jnp.where((k >= HALF) & (x == 0), 1.0, 0.0)
    W[cols : cols + 128, 0:cols] = diff.astype(BF16)
    k, x = iota((cols, 128), 0), iota((cols, 128), 1)
    E[...] = jnp.where(((k == 0) & (x < HALF)) | ((k == cols - 1) & (x >= HALF)), 1.0, 0.0).astype(BF16)
    m, k = iota((4 * RU, 12 * RU), 0), iota((4 * RU, 12 * RU), 1)
    at = (m // RU) * (3 * RU) + RU + lax.rem(m, RU)
    A[...] = (jnp.where(k == at + 1, 1.0, 0.0) - jnp.where(k == at - 1, 1.0, 0.0)).astype(BF16)
    for n, t in enumerate(tables(tf, total_depth)):
        tab[n] = t

    lane_half = lax.rem(iota((RU, 128), 1), HALF)
    lane_halo = iota((RU, 128), 1)
    keep_right = jnp.where(gx == n_gx - 1, 0.0, 1.0)
    keep_left = jnp.where(gx == 0, 0.0, 1.0)

    def extract(u):
        load(u).wait()
        y0 = unit_rows(u)
        for part in range(2):
            block = D[part * HALF : (part + 1) * HALF, pl.ds(RU + y0, RU), :].reshape(HALF * RU, cols)
            spread = dot(block, E[...])
            acc = jnp.zeros((RU, 128), F32)
            for z in range(HALF):
                acc = jnp.where(lane_half == z, spread[z * RU : (z + 1) * RU], acc)
            edge[u, part] = acc.astype(BF16)

    def halo_copies(u):
        return [
            pltpu.make_async_remote_copy(
                src_ref=edge.at[u], dst_ref=halo_in.at[side, u], send_sem=halo_ssem.at[side, u],
                recv_sem=halo_rsem.at[side, u], device_id=(target, gz), device_id_type=MESH,
            )
            for side, target in ((0, left), (1, right))
        ]

    def halo_arrive(u):
        for copy in halo_copies(u):
            copy.wait()
        for part in range(2):
            halo[u, part] = jnp.where(
                lane_halo < HALF,
                halo_in[0, u, part].astype(F32) * keep_right,
                halo_in[1, u, part].astype(F32) * keep_left,
            ).astype(BF16)

    extract(0)
    pl.semaphore_wait(barrier, len(peers))
    for copy in halo_copies(0):
        copy.start()

    def send_edges(u, _):
        extract(u)
        for copy in halo_copies(u):
            copy.start()
        return 0

    lax.fori_loop(1, UNITS, send_edges, 0)
    halo_arrive(0)

    def slopes(u, zb, pb, rb):
        y0 = unit_rows(u)
        z0 = pl.multiple_of(zb * ZB, ZB)
        block = D[pl.ds(z0, ZB), pl.ds(RU + y0, RU), :].reshape(ZB * RU, cols)
        part = z0 // HALF
        edges = halo[u, part][None] * onehot[pl.ds(z0 - part * HALF, ZB)]
        lhs = jnp.concatenate([block, edges.reshape(ZB * RU, 128)], 1)
        pb[0] = dot(lhs, W[:, 0:cols])
        pb[1] = dot(block, W[0:cols, cols : 2 * cols])
        for i in range(ZB // 4):
            near = D[pl.ds(z0 + 4 * i, 4), pl.ds(y0, 3 * RU), :].reshape(12 * RU, cols)
            rb[4 * RU * i : 4 * RU * (i + 1), :] = dot(A[...], near)

    def march(y0, zb, pb, rb, carry):
        z0 = zb * ZB
        T = [tab[n] for n in range(8)]

        def step(i, z, carry):
            r0 = pl.multiple_of(z * RU + 8 * i, 8)
            dx, dens = [pb[n, pl.ds(r0, 8)] for n in range(2)]
            dy = rb[pl.ds(r0, 8)]
            new = []
            for j in range(2):
                sl = (slice(0, 8), slice(128 * j, 128 * j + 128))
                p, r, d = dx[sl], dy[sl], dens[sl]
                run, clear, red, green, blue = carry[5 * j : 5 * j + 5]
                q = (0.75 * p + r) * lax.rsqrt(p * p + (r * r + 0.0625))
                ix = d.astype(jnp.int32)
                run = run + (look(T[6], ix) + look(T[7], ix) * d)
                after = jnp.exp2(run)
                w = (clear - after) * (1.25 + q)
                red = red + w * (look(T[0], ix) + look(T[1], ix) * d)
                green = green + w * (look(T[2], ix) + look(T[3], ix) * d)
                blue = blue + w * (look(T[4], ix) + look(T[5], ix) * d)
                new += [run, after, red, green, blue]
            return tuple(new)

        halves = []
        for i in range(2):
            halves += lax.fori_loop(0, ZB, functools.partial(step, i), carry[10 * i : 10 * i + 10], unroll=True)
        return tuple(halves)

    def strip_copy(u):
        slot = u // 4
        target = lax.rem(gz + 1 + lax.rem(u, 4), 4)
        return pltpu.make_async_remote_copy(
            src_ref=strip.at[u], dst_ref=bricks.at[slot, gz], send_sem=strip_ssem.at[u],
            recv_sem=strip_rsem.at[slot, gz], device_id=(gx, target), device_id_type=MESH,
        )

    first, second = (z_peers, x_peers), (x_peers, z_peers)

    def place(h, p, k, j, c):
        x, z = lax.rem(chip_x + (j if p else k), 4), lax.rem(chip_z + (k if p else j), 4)
        at = pl.multiple_of(gx_of(x, z, c) * cols, cols)
        return out.at[2 * p : 2 * p + 2, RU * h : RU * h + RU, pl.ds(at, cols)]

    def own_copy(h):
        at = pl.multiple_of(gx * cols, cols)
        return pltpu.make_async_copy(blk.at[h], out.at[:, RU * h : RU * h + RU, pl.ds(at, cols)], own_sem.at[h])

    def held(h, p, k, j):
        return blk.at[h, 2 * p : 2 * p + 2] if k == 0 and j == 0 else place(h, p, k, j, core)

    def send(src, dst, ssem, rsem, target):
        return pltpu.make_async_remote_copy(
            src_ref=src, dst_ref=dst, send_sem=ssem, recv_sem=rsem, device_id=target, device_id_type=MESH
        )

    def a_copy(h, p, m):
        return send(held(h, p, 0, 0), place(h, p, 0, 0, core), a_ssem.at[h, p, m - 1], a_rsem.at[h, p, m - 1], first[p][m - 1])

    def a_arrival(h, p, j):
        spot = place(h, p, 0, j, core)
        return send(spot, spot, a_ssem.at[h, p, 3 - j], a_rsem.at[h, p, 3 - j], first[p][3 - j])

    def b_copy(h, p, m, j):
        return send(held(h, p, 0, j), place(h, p, 0, j, core), b_ssem.at[h, p, m - 1, j], b_rsem.at[h, p, m - 1, j], second[p][m - 1])

    def b_arrival(h, p, k, j):
        spot = place(h, p, k, j, core)
        return send(spot, spot, b_ssem.at[h, p, 3 - k, j], b_rsem.at[h, p, 3 - k, j], second[p][3 - k])

    def c_copy(h, p, k, j):
        return send(held(h, p, k, j), place(h, p, k, j, core), c_ssem.at[h, p, k, j], c_rsem.at[h, p, k, j], sibling)

    def c_arrival(h, p, k, j):
        spot = place(h, p, k, j, 1 - core)
        return send(spot, spot, c_ssem.at[h, p, k, j], c_rsem.at[h, p, k, j], sibling)

    NEAR = (1, 3, 2)

    def composite(h):
        for k in (1, 2, 3):
            brick = lax.rem(gz + k, 4)
            pltpu.make_async_remote_copy(
                src_ref=strip.at[0], dst_ref=bricks.at[h, brick], send_sem=strip_ssem.at[0],
                recv_sem=strip_rsem.at[h, brick], device_id=(gx, brick), device_id_type=MESH,
            ).wait_recv()
        ahead = bricks[h, 0, 3]
        total = [bricks[h, 0, c] for c in range(3)] + [1.0 - ahead]
        for b in range(1, 4):
            through = bricks[h, b, 3]
            total = [total[c] + ahead * bricks[h, b, c] for c in range(3)] + [total[3] + ahead * (1.0 - through)]
            ahead = ahead * through
        for c in range(4):
            blk[h, c] = total[c].astype(BF16)
        for p in range(2):
            for m in NEAR:
                a_copy(h, p, m).start()
        for p in range(2):
            for m in NEAR:
                b_copy(h, p, m, 0).start()
        own_copy(h).start()
        for p in range(2):
            c_copy(h, p, 0, 0).start()

    def stage_b(h):
        own_copy(h).wait()
        for j in NEAR:
            for p in range(2):
                a_arrival(h, p, j).wait_recv()
                for m in NEAR:
                    b_copy(h, p, m, j).start()
                c_copy(h, p, 0, j).start()

    def stage_c(h):
        for j in (0,) + NEAR:
            for k in NEAR:
                for p in range(2):
                    b_arrival(h, p, k, j).wait_recv()
                    c_copy(h, p, k, j).start()

    def unit(u, _):
        y0 = unit_rows(u)
        zero, one = jnp.zeros((8, 128), F32), jnp.ones((8, 128), F32)

        def blocks(i, carry):
            @pl.when((i == NZB // AHEAD - 2) & (u < UNITS - 1))
            def _():
                halo_arrive(u + 1)

            for n in range(AHEAD):
                carry = march(y0, AHEAD * i + n, pb.at[n], rb.at[n], carry)
                ahead = AHEAD * (i + 1) + n
                later = jnp.minimum(u + ahead // NZB, UNITS - 1)
                slopes(later, lax.rem(ahead, NZB), pb.at[n], rb.at[n])
            return carry

        carry = lax.fori_loop(0, NZB // AHEAD, blocks, (zero, one, zero, zero, zero) * 4)

        def keep(ref):
            for k in range(4):
                i, j = k // 2, k % 2
                _, clear, red, green, blue = carry[5 * k : 5 * k + 5]
                for c, v in enumerate((red, green, blue, clear)):
                    ref[c, 8 * i : 8 * i + 8, 128 * j : 128 * j + 128] = v

        @pl.when(lax.rem(u, 4) < 3)
        def _():
            keep(strip.at[u])
            strip_copy(u).start()

        @pl.when(lax.rem(u, 4) == 3)
        def _():
            keep(bricks.at[u // 4, gz])

        @pl.when(u == 4)
        def _():
            composite(0)

        @pl.when(u == 5)
        def _():
            stage_b(0)

        @pl.when(u == 6)
        def _():
            stage_c(0)

        return 0

    for n in range(AHEAD):
        slopes(0, n, pb.at[n], rb.at[n])
    lax.fori_loop(0, UNITS, unit, 0)
    def finish(h):
        for p in range(2):
            for j in range(4):
                for k in range(4):
                    c_arrival(h, p, k, j).wait_recv()
                    c_copy(h, p, k, j).wait_send()

    def sent(h):
        for p in range(2):
            for m in range(1, 4):
                for j in range(4):
                    b_copy(h, p, m, j).wait_send()
                a_copy(h, p, m).wait_send()
        for i in range(3):
            strip_copy(4 * h + i).wait_send()

    composite(1)
    finish(0)
    stage_b(1)
    sent(0)
    stage_c(1)
    sent(1)
    finish(1)


def render(density, tf_color, tf_extinction):
    depth, rows, cols = density.shape
    n_gx, n_gz = lax.axis_size("gx"), lax.axis_size("gz")
    D = pltpu.SemaphoreType.DMA
    return pl.pallas_call(
        functools.partial(kernel, depth * n_gz),
        out_shape=jax.ShapeDtypeStruct((4, rows // n_gz, cols * n_gx), BF16),
        in_specs=[
            pl.BlockSpec(memory_space=pl.ANY),
            pl.BlockSpec(memory_space=pltpu.SMEM),
        ],
        out_specs=pl.BlockSpec(memory_space=pl.ANY),
        scratch_shapes=[
            pltpu.VMEM((depth, rows + 2 * RU, cols), BF16),
            pltpu.VMEM((depth // 2, RU, 128), BF16),
            pltpu.VMEM((UNITS, 2, RU, 128), BF16),
            pltpu.VMEM((2, UNITS, 2, RU, 128), BF16),
            pltpu.VMEM((UNITS, 2, RU, 128), BF16),
            pltpu.VMEM((cols + 128, 2 * cols), BF16),
            pltpu.VMEM((4 * RU, 12 * RU), BF16),
            pltpu.VMEM((cols, 128), BF16),
            pltpu.VMEM((8, 8, 128), F32),
            pltpu.VMEM((AHEAD, 2, ZB * RU, cols), F32),
            pltpu.VMEM((AHEAD, ZB * RU, cols), F32),
            pltpu.VMEM((4 * ROUNDS, 4, RU, cols), F32),
            pltpu.VMEM((ROUNDS, 4, 4, RU, cols), F32),
            pltpu.VMEM((ROUNDS, 4, RU, cols), BF16),
            D((UNITS,)),
            D((2, UNITS)),
            D((2, UNITS)),
            D((UNITS,)),
            D((ROUNDS, 4)),
            D((ROUNDS,)),
            D((ROUNDS, 2, 3)),
            D((ROUNDS, 2, 3)),
            D((ROUNDS, 2, 3, 4)),
            D((ROUNDS, 2, 3, 4)),
            D((ROUNDS, 2, 4, 4)),
            D((ROUNDS, 2, 4, 4)),
        ],
        compiler_params=pltpu.CompilerParams(
            collective_id=0, has_side_effects=True, vmem_limit_bytes=50 * 2**20
        ),
    )(density, jnp.concatenate([tf_color, tf_extinction[None]], 0))


def solution(mesh):
    in_specs = (P("gz", None, "gx"), P(), P())
    return jax.shard_map(
        render, mesh=mesh, in_specs=in_specs, out_specs=P(None, "gz", None), check_vma=False
    )
```

```python
import functools
import math

import jax
import jax.numpy as jnp
from jax import lax
from jax.experimental import pallas as pl
from jax.experimental.pallas import tpu as pltpu
from jax.sharding import PartitionSpec as P

F32, BF16 = jnp.float32, jnp.bfloat16
MESH = pl.DeviceIdType.MESH
RU = 16
AHEAD = 8
ZB = 8
ROUNDS = 2
UNITS = 4 * ROUNDS
GATHER = lax.GatherDimensionNumbers(
    offset_dims=(),
    collapsed_slice_dims=(0,),
    start_index_map=(0,),
    operand_batching_dims=(1,),
    start_indices_batching_dims=(1,),
)


def look(table, index):
    return lax.gather(
        table, index[..., None], GATHER, (1, 1), mode=lax.GatherScatterMode.PROMISE_IN_BOUNDS
    )


def dot(a, b):
    return jnp.dot(a, b, preferred_element_type=F32)


def iota(shape, dim):
    return lax.broadcasted_iota(jnp.int32, shape, dim)


def tables(tf, total_depth):
    knots = tf.shape[1]
    row = iota((8, 128), 0)
    found = []
    for fn in range(4):
        scale = 0.4 if fn < 3 else -math.log2(math.e) / total_depth
        value = [tf[fn, k] * scale for k in range(knots)]
        a = jnp.zeros((8, 128), F32)
        b = jnp.zeros((8, 128), F32)
        for k in range(knots):
            if k + 1 < knots:
                rise = value[k + 1] - value[k]
                a = jnp.where(row == k, value[k] - rise * float(k), a)
                b = jnp.where(row == k, rise, b)
            else:
                a = jnp.where(row == k, value[k], a)
        found += [a, b]
    return found


def kernel(
    total_depth, den, tf, out,
    D, onehot, edge, halo_in, halo, W, A, E, tab, pb, rb, strip, bricks, blk,
    load_sem, halo_ssem, halo_rsem, strip_ssem, strip_rsem, own_sem,
    a_ssem, a_rsem, b_ssem, b_rsem, c_ssem, c_rsem,
):
    gx, gz = lax.axis_index("gx"), lax.axis_index("gz")
    n_gx, n_gz = lax.axis_size("gx"), lax.axis_size("gz")
    depth, rows, cols = den.shape
    core, chip_z, chip_x = lax.rem(gx, 2), lax.rem(gx // 2, 4), gx // 8
    NZB = depth // ZB
    HALF = depth // 2

    def gx_of(x, z, c):
        return x * 8 + z * 2 + c

    def unit_rows(u):
        return pl.multiple_of(lax.rem(gz + 1 + lax.rem(u, 4), 4) * (2 * RU) + (u // 4) * RU, RU)

    def load(u):
        y0 = unit_rows(u)
        return pltpu.make_async_copy(
            den.at[:, pl.ds(y0, RU), :], D.at[:, pl.ds(RU + y0, RU), :], load_sem.at[u]
        )

    def begin_load(u, _):
        load(u).start()
        return 0

    load(0).start()

    left, right = lax.rem(gx + n_gx - 1, n_gx), lax.rem(gx + 1, n_gx)
    sibling = (gx_of(chip_x, chip_z, 1 - core), gz)
    z_peers = [(gx_of(chip_x, lax.rem(chip_z + k, 4), core), gz) for k in (1, 2, 3)]
    x_peers = [(gx_of(lax.rem(chip_x + k, 4), chip_z, core), gz) for k in (1, 2, 3)]
    y_peers = [(gx, lax.rem(gz + k, n_gz)) for k in (1, 2, 3)]
    barrier = pltpu.get_barrier_semaphore()
    peers = [(left, gz), (right, gz), sibling] + z_peers + x_peers + y_peers
    for peer in peers:
        pl.semaphore_signal(barrier, inc=1, device_id=peer, device_id_type=MESH)
    lax.fori_loop(1, UNITS, begin_load, 0)

    D[:, 0:RU, :] = jnp.zeros((depth, RU, cols), BF16)
    D[:, RU + rows : 2 * RU + rows, :] = jnp.zeros((depth, RU, cols), BF16)
    lane = lax.rem(iota((RU, 128), 1), HALF)

    def mark(z, _):
        onehot[z] = jnp.where(lane == z, 1.0, 0.0).astype(BF16)
        return 0

    lax.fori_loop(0, HALF, mark, 0)
    k, x = iota((cols, cols), 0), iota((cols, cols), 1)
    diff = jnp.where(k == x + 1, 1.0, 0.0) - jnp.where(k == x - 1, 1.0, 0.0)
    W[0:cols, 0:cols] = diff.astype(BF16)
    W[0:cols, cols : 2 * cols] = jnp.where(k == x, 7.0, 0.0).astype(BF16)
    k, x = iota((128, cols), 0), iota((128, cols), 1)
    diff = jnp.where((k < HALF) & (x == cols - 1), 1.0, 0.0) - jnp.where((k >= HALF) & (x == 0), 1.0, 0.0)
    W[cols : cols + 128, 0:cols] = diff.astype(BF16)
    k, x = iota((cols, 128), 0), iota((cols, 128), 1)
    E[...] = jnp.where(((k == 0) & (x < HALF)) | ((k == cols - 1) & (x >= HALF)), 1.0, 0.0).astype(BF16)
    m, k = iota((4 * RU, 12 * RU), 0), iota((4 * RU, 12 * RU), 1)
    at = (m // RU) * (3 * RU) + RU + lax.rem(m, RU)
    A[...] = (jnp.where(k == at + 1, 1.0, 0.0) - jnp.where(k == at - 1, 1.0, 0.0)).astype(BF16)
    for n, t in enumerate(tables(tf, total_depth)):
        tab[n] = t

    lane_half = lax.rem(iota((RU, 128), 1), HALF)
    lane_halo = iota((RU, 128), 1)
    keep_right = jnp.where(gx == n_gx - 1, 0.0, 1.0)
    keep_left = jnp.where(gx == 0, 0.0, 1.0)

    def extract(u):
        load(u).wait()
        y0 = unit_rows(u)
        for part in range(2):
            block = D[part * HALF : (part + 1) * HALF, pl.ds(RU + y0, RU), :].reshape(HALF * RU, cols)
            spread = dot(block, E[...])
            acc = jnp.zeros((RU, 128), F32)
            for z in range(HALF):
                acc = jnp.where(lane_half == z, spread[z * RU : (z + 1) * RU], acc)
            edge[u, part] = acc.astype(BF16)

    def halo_copies(u):
        return [
            pltpu.make_async_remote_copy(
                src_ref=edge.at[u], dst_ref=halo_in.at[side, u], send_sem=halo_ssem.at[side, u],
                recv_sem=halo_rsem.at[side, u], device_id=(target, gz), device_id_type=MESH,
            )
            for side, target in ((0, left), (1, right))
        ]

    def halo_arrive(u):
        for copy in halo_copies(u):
            copy.wait()
        for part in range(2):
            halo[u, part] = jnp.where(
                lane_halo < HALF,
                halo_in[0, u, part].astype(F32) * keep_right,
                halo_in[1, u, part].astype(F32) * keep_left,
            ).astype(BF16)

    extract(0)
    pl.semaphore_wait(barrier, len(peers))
    for copy in halo_copies(0):
        copy.start()

    def send_edges(u, _):
        extract(u)
        for copy in halo_copies(u):
            copy.start()
        return 0

    lax.fori_loop(1, UNITS, send_edges, 0)
    halo_arrive(0)

    def slopes(u, zb, pb, rb):
        y0 = unit_rows(u)
        z0 = pl.multiple_of(zb * ZB, ZB)
        block = D[pl.ds(z0, ZB), pl.ds(RU + y0, RU), :].reshape(ZB * RU, cols)
        part = z0 // HALF
        edges = halo[u, part][None] * onehot[pl.ds(z0 - part * HALF, ZB)]
        lhs = jnp.concatenate([block, edges.reshape(ZB * RU, 128)], 1)
        pb[0] = dot(lhs, W[:, 0:cols])
        pb[1] = dot(block, W[0:cols, cols : 2 * cols])
        for i in range(ZB // 4):
            near = D[pl.ds(z0 + 4 * i, 4), pl.ds(y0, 3 * RU), :].reshape(12 * RU, cols)
            rb[4 * RU * i : 4 * RU * (i + 1), :] = dot(A[...], near)

    def march(y0, zb, pb, rb, carry):
        z0 = zb * ZB
        T = [tab[n] for n in range(8)]

        def step(i, z, carry):
            r0 = pl.multiple_of(z * RU + 8 * i, 8)
            dx, dens = [pb[n, pl.ds(r0, 8)] for n in range(2)]
            dy = rb[pl.ds(r0, 8)]
            new = []
            for j in range(2):
                sl = (slice(0, 8), slice(128 * j, 128 * j + 128))
                p, r, d = dx[sl], dy[sl], dens[sl]
                run, clear, red, green, blue = carry[5 * j : 5 * j + 5]
                q = (0.75 * p + r) * lax.rsqrt(p * p + (r * r + 0.0625))
                ix = d.astype(jnp.int32)
                run = run + (look(T[6], ix) + look(T[7], ix) * d)
                after = jnp.exp2(run)
                w = (clear - after) * (1.25 + q)
                red = red + w * (look(T[0], ix) + look(T[1], ix) * d)
                green = green + w * (look(T[2], ix) + look(T[3], ix) * d)
                blue = blue + w * (look(T[4], ix) + look(T[5], ix) * d)
                new += [run, after, red, green, blue]
            return tuple(new)

        halves = []
        for i in range(2):
            halves += lax.fori_loop(0, ZB, functools.partial(step, i), carry[10 * i : 10 * i + 10], unroll=True)
        return tuple(halves)

    def strip_copy(u):
        slot = u // 4
        target = lax.rem(gz + 1 + lax.rem(u, 4), 4)
        return pltpu.make_async_remote_copy(
            src_ref=strip.at[u], dst_ref=bricks.at[slot, gz], send_sem=strip_ssem.at[u],
            recv_sem=strip_rsem.at[slot, gz], device_id=(gx, target), device_id_type=MESH,
        )

    first, second = (z_peers, x_peers), (x_peers, z_peers)

    def place(h, p, k, j, c):
        x, z = lax.rem(chip_x + (j if p else k), 4), lax.rem(chip_z + (k if p else j), 4)
        at = pl.multiple_of(gx_of(x, z, c) * cols, cols)
        return out.at[2 * p : 2 * p + 2, RU * h : RU * h + RU, pl.ds(at, cols)]

    def own_copy(h):
        at = pl.multiple_of(gx * cols, cols)
        return pltpu.make_async_copy(blk.at[h], out.at[:, RU * h : RU * h + RU, pl.ds(at, cols)], own_sem.at[h])

    def held(h, p, k, j):
        return blk.at[h, 2 * p : 2 * p + 2] if k == 0 and j == 0 else place(h, p, k, j, core)

    def send(src, dst, ssem, rsem, target):
        return pltpu.make_async_remote_copy(
            src_ref=src, dst_ref=dst, send_sem=ssem, recv_sem=rsem, device_id=target, device_id_type=MESH
        )

    def a_copy(h, p, m):
        return send(held(h, p, 0, 0), place(h, p, 0, 0, core), a_ssem.at[h, p, m - 1], a_rsem.at[h, p, m - 1], first[p][m - 1])

    def a_arrival(h, p, j):
        spot = place(h, p, 0, j, core)
        return send(spot, spot, a_ssem.at[h, p, 3 - j], a_rsem.at[h, p, 3 - j], first[p][3 - j])

    def b_copy(h, p, m, j):
        return send(held(h, p, 0, j), place(h, p, 0, j, core), b_ssem.at[h, p, m - 1, j], b_rsem.at[h, p, m - 1, j], second[p][m - 1])

    def b_arrival(h, p, k, j):
        spot = place(h, p, k, j, core)
        return send(spot, spot, b_ssem.at[h, p, 3 - k, j], b_rsem.at[h, p, 3 - k, j], second[p][3 - k])

    def c_copy(h, p, k, j):
        return send(held(h, p, k, j), place(h, p, k, j, core), c_ssem.at[h, p, k, j], c_rsem.at[h, p, k, j], sibling)

    def c_arrival(h, p, k, j):
        spot = place(h, p, k, j, 1 - core)
        return send(spot, spot, c_ssem.at[h, p, k, j], c_rsem.at[h, p, k, j], sibling)

    NEAR = (1, 3, 2)

    def composite(h):
        for k in (1, 2, 3):
            brick = lax.rem(gz + k, 4)
            pltpu.make_async_remote_copy(
                src_ref=strip.at[0], dst_ref=bricks.at[h, brick], send_sem=strip_ssem.at[0],
                recv_sem=strip_rsem.at[h, brick], device_id=(gx, brick), device_id_type=MESH,
            ).wait_recv()
        ahead = bricks[h, 0, 3]
        total = [bricks[h, 0, c] for c in range(3)] + [1.0 - ahead]
        for b in range(1, 4):
            through = bricks[h, b, 3]
            total = [total[c] + ahead * bricks[h, b, c] for c in range(3)] + [total[3] + ahead * (1.0 - through)]
            ahead = ahead * through
        for c in range(4):
            blk[h, c] = total[c].astype(BF16)
        for p in range(2):
            for m in NEAR:
                a_copy(h, p, m).start()
        for p in range(2):
            for m in NEAR:
                b_copy(h, p, m, 0).start()
        own_copy(h).start()
        for p in range(2):
            c_copy(h, p, 0, 0).start()

    def stage_b(h):
        own_copy(h).wait()
        for j in NEAR:
            for p in range(2):
                a_arrival(h, p, j).wait_recv()
                for m in NEAR:
                    b_copy(h, p, m, j).start()
                c_copy(h, p, 0, j).start()

    def stage_c(h):
        for j in (0,) + NEAR:
            for k in NEAR:
                for p in range(2):
                    b_arrival(h, p, k, j).wait_recv()
                    c_copy(h, p, k, j).start()

    def unit(u, _):
        y0 = unit_rows(u)
        zero, one = jnp.zeros((8, 128), F32), jnp.ones((8, 128), F32)

        def blocks(i, carry):
            @pl.when((i == NZB // AHEAD - 2) & (u < UNITS - 1))
            def _():
                halo_arrive(u + 1)

            for n in range(AHEAD):
                carry = march(y0, AHEAD * i + n, pb.at[n], rb.at[n], carry)
                ahead = AHEAD * (i + 1) + n
                later = jnp.minimum(u + ahead // NZB, UNITS - 1)
                slopes(later, lax.rem(ahead, NZB), pb.at[n], rb.at[n])
            return carry

        carry = lax.fori_loop(0, NZB // AHEAD, blocks, (zero, one, zero, zero, zero) * 4)

        def keep(ref):
            for k in range(4):
                i, j = k // 2, k % 2
                _, clear, red, green, blue = carry[5 * k : 5 * k + 5]
                for c, v in enumerate((red, green, blue, clear)):
                    ref[c, 8 * i : 8 * i + 8, 128 * j : 128 * j + 128] = v

        @pl.when(lax.rem(u, 4) < 3)
        def _():
            keep(strip.at[u])
            strip_copy(u).start()

        @pl.when(lax.rem(u, 4) == 3)
        def _():
            keep(bricks.at[u // 4, gz])

        @pl.when(u == 4)
        def _():
            composite(0)

        @pl.when(u == 5)
        def _():
            stage_b(0)

        @pl.when(u == 6)
        def _():
            stage_c(0)

        return 0

    for n in range(AHEAD):
        slopes(0, n, pb.at[n], rb.at[n])
    lax.fori_loop(0, UNITS, unit, 0)
    def finish(h):
        for p in range(2):
            for j in range(4):
                for k in range(4):
                    c_arrival(h, p, k, j).wait_recv()
                    c_copy(h, p, k, j).wait_send()

    def sent(h):
        for p in range(2):
            for m in range(1, 4):
                for j in range(4):
                    b_copy(h, p, m, j).wait_send()
                a_copy(h, p, m).wait_send()
        for i in range(3):
            strip_copy(4 * h + i).wait_send()

    composite(1)
    finish(0)
    stage_b(1)
    sent(0)
    stage_c(1)
    sent(1)
    finish(1)


def render(density, tf_color, tf_extinction):
    depth, rows, cols = density.shape
    n_gx, n_gz = lax.axis_size("gx"), lax.axis_size("gz")
    D = pltpu.SemaphoreType.DMA
    return pl.pallas_call(
        functools.partial(kernel, depth * n_gz),
        out_shape=jax.ShapeDtypeStruct((4, rows // n_gz, cols * n_gx), BF16),
        in_specs=[
            pl.BlockSpec(memory_space=pl.ANY),
            pl.BlockSpec(memory_space=pltpu.SMEM),
        ],
        out_specs=pl.BlockSpec(memory_space=pl.ANY),
        scratch_shapes=[
            pltpu.VMEM((depth, rows + 2 * RU, cols), BF16),
            pltpu.VMEM((depth // 2, RU, 128), BF16),
            pltpu.VMEM((UNITS, 2, RU, 128), BF16),
            pltpu.VMEM((2, UNITS, 2, RU, 128), BF16),
            pltpu.VMEM((UNITS, 2, RU, 128), BF16),
            pltpu.VMEM((cols + 128, 2 * cols), BF16),
            pltpu.VMEM((4 * RU, 12 * RU), BF16),
            pltpu.VMEM((cols, 128), BF16),
            pltpu.VMEM((8, 8, 128), F32),
            pltpu.VMEM((AHEAD, 2, ZB * RU, cols), F32),
            pltpu.VMEM((AHEAD, ZB * RU, cols), F32),
            pltpu.VMEM((4 * ROUNDS, 4, RU, cols), F32),
            pltpu.VMEM((ROUNDS, 4, 4, RU, cols), F32),
            pltpu.VMEM((ROUNDS, 4, RU, cols), BF16),
            D((UNITS,)),
            D((2, UNITS)),
            D((2, UNITS)),
            D((UNITS,)),
            D((ROUNDS, 4)),
            D((ROUNDS,)),
            D((ROUNDS, 2, 3)),
            D((ROUNDS, 2, 3)),
            D((ROUNDS, 2, 3, 4)),
            D((ROUNDS, 2, 3, 4)),
            D((ROUNDS, 2, 4, 4)),
            D((ROUNDS, 2, 4, 4)),
        ],
        compiler_params=pltpu.CompilerParams(
            collective_id=0, has_side_effects=True, vmem_limit_bytes=50 * 2**20
        ),
    )(density, jnp.concatenate([tf_color, tf_extinction[None]], 0))


def solution(mesh):
    in_specs = (P("gz", None, "gx"), P(), P())
    return jax.shard_map(
        render, mesh=mesh, in_specs=in_specs, out_specs=P(None, "gz", None), check_vma=False
    )
```
